32 devices in a mesh: parts: 2 (over y), seq: 8 (over z, x), head: 2 (over core).
Axes of the slice: x: 2, y: 2, z: 4, core: 2. Of those that a mesh axis runs over, the one named last changes fastest.
Arguments:
- query_states: bfloat16 [4096, 8192], P(('parts', 'seq', 'head')), parts along dimension 0, may hold values from -80 to 80, as said below
- key_states: bfloat16 [4096, 1024], P(('parts', 'seq', 'head')), parts along dimension 0, may hold values from -6 to 6
- value_states: bfloat16 [4096, 1024], P(('parts', 'seq', 'head')), parts along dimension 0, may hold values from -12 to 12
- vertical_blocks: int32 [16, 6], P('parts'), parts along dimension 0, may hold values from 0 to 31, as said below
- slash_offsets: int32 [16, 6], P('parts'), parts along dimension 0, may hold values from 0 to 7, as said below
Outputs:
- attended: bfloat16 [4096, 8192], P(('parts', 'seq', 'head')), parts along dimension 0
The draws below stay inside these ranges and needn't reach their ends.
There are 2 independent parts, one for each index of `parts`. The reference program is written for one: setup_inputs(seed, part) draws one part's arguments, and reference() takes and returns one part's arrays. A program takes and returns all parts, laid end to end along the dimension named above; each array names one. Nothing has to cross between parts.
Inputs may be any that keep to these rules, and one draw needn't show every extreme that they name: `query_states`: entries of order one, a few larger. `vertical_blocks`: each row lists 6 different key blocks, among them block 0. `slash_offsets`: each row lists 6 different block offsets, among them 0 and 1.
All inputs are finite; a program needn't handle non-finite values.
Results may differ from the reference program's by a relative error of at most 0.0034.
Values may be sent and summed in bfloat16 or wider, within the bound.
A program may use at most 64 MiB of HBM per device.

```python
import math
import jax
import jax.numpy as jnp
from jax import lax

QH = 64
KVH = 8
HD = 128
TOK_DEV = 256
BS = 64
NS = 6
NV = 6
S = 2048
QB = 32
SPAN = 8


def draw_states(key):
    folded = jax.random.fold_in(key, 7)
    key_stream, query_stream = jax.random.split(folded)
    groups = QH // KVH
    key_field = jnp.clip(jax.random.normal(key_stream, (S, KVH, HD), jnp.float32), -6.0, 6.0)
    query_field = jnp.clip(2.0 * jax.random.normal(query_stream, (S, KVH, groups, HD), jnp.float32), -12.0, 12.0)
    query_field = jnp.clip(query_field, -80.0, 80.0)
    return (query_field.reshape(S, QH * HD), jnp.clip(key_field, -6.0, 6.0).reshape(S, KVH * HD))


def draw_query_states(key, part):
    return draw_states(key)[0].astype(jnp.bfloat16)


def draw_key_states(key, part):
    return draw_states(key)[1].astype(jnp.bfloat16)


def draw_vertical_blocks(key, part):
    folded = jax.random.fold_in(key, 11)
    streams = jax.random.split(folded, KVH)

    def per_head(stream):
        chosen = jax.random.permutation(stream, QB - 2)[:NV - 2] + 1
        return jnp.concatenate([jnp.array([0, QB - 1], jnp.int32), chosen.astype(jnp.int32)])
    return jax.vmap(per_head)(streams)


def draw_slash_offsets(key, part):
    folded = jax.random.fold_in(key, 13)
    streams = jax.random.split(folded, KVH)

    def per_head(stream):
        chosen = jax.random.permutation(stream, SPAN - 3)[:NS - 3] + 2
        return jnp.concatenate([jnp.array([0, 1, SPAN - 1], jnp.int32), chosen.astype(jnp.int32)])
    return jax.vmap(per_head)(streams)


def block_scale(rng, shape, shards, least, top_value):
    gain, own = 1.0, jax.random.fold_in(rng, 6)
    for dim, parts in shards:
        draws = jnp.exp(jax.random.uniform(jax.random.fold_in(own, dim), (parts,), jnp.float32, least / len(shards), top_value / len(shards)))
        gain = gain * jnp.repeat(draws, shape[dim] // parts).reshape([-1 if axis == dim else 1 for axis in range(len(shape))])
    return gain


def bell_draw(stream_key, shape, deviation, most, shards=(), kind=jnp.bfloat16):
    values = deviation * jax.random.normal(stream_key, shape, jnp.float32)
    if shards:
        values = values * block_scale(stream_key, shape, shards, -0.22, 0.18)
    return jnp.clip(values, -most, most).astype(kind)


def setup_inputs(seed: int = 0, part: int = 0) -> dict:
    key_list = jax.random.split(jax.random.key(seed), 6)
    part_splits = jax.random.split(jax.random.fold_in(key_list[5], part), 6)
    query_states = draw_query_states(jax.random.fold_in(jax.random.fold_in(key_list[5], part), 71), part)
    key_states = draw_key_states(jax.random.fold_in(jax.random.fold_in(key_list[5], part), 71), part)
    value_states = bell_draw(part_splits[2], (S, KVH * HD), 2.0, 12.0, ((0, 16),))
    vertical_blocks = draw_vertical_blocks(jax.random.fold_in(jax.random.fold_in(key_list[5], part), 71), part)
    slash_offsets = draw_slash_offsets(jax.random.fold_in(jax.random.fold_in(key_list[5], part), 71), part)
    return {"query_states": query_states, "key_states": key_states, "value_states": value_states, "vertical_blocks": vertical_blocks, "slash_offsets": slash_offsets}


def block_mask(query_block, slash_here, vertical_here):
    positions = jnp.arange(BS, dtype=jnp.int32)
    causal = positions[None, :] <= positions[:, None]
    key_block = query_block - slash_here
    slash_ok = (key_block >= 0)[:, :, None, None] & ((slash_here != 0)[:, :, None, None] | causal[None, None])
    slash_ok = jnp.transpose(slash_ok, (0, 2, 1, 3)).reshape(slash_here.shape[0], BS, -1)
    on_slash = jnp.any((query_block - vertical_here)[:, :, None] == slash_here[:, None, :], axis=-1)
    vertical_ok = (vertical_here <= query_block) & jnp.logical_not(on_slash)
    vertical_ok = jnp.broadcast_to(vertical_ok[:, None, :, None], (vertical_here.shape[0], BS, vertical_here.shape[1], BS))
    vertical_ok = vertical_ok.reshape(vertical_here.shape[0], BS, -1)
    return jnp.concatenate([slash_ok, vertical_ok], axis=-1)

def attend_block(query_tile, key_rows, value_rows, active, score_scale):
    scores = jnp.einsum('tgch,gkh->gctk', query_tile.astype(jnp.float32), key_rows.astype(jnp.float32)) * score_scale
    scores = jnp.where(active[:, None], scores, -jnp.inf)
    row_max = lax.optimization_barrier(jnp.max(scores, axis=-1, keepdims=True))
    weights = jnp.exp(scores - row_max)
    row_total = lax.optimization_barrier(jnp.sum(weights, axis=-1))
    rounded = weights.astype(jnp.bfloat16)
    mixed_rows = jnp.einsum('gctk,gkh->tgch', rounded.astype(jnp.float32), value_rows.astype(jnp.float32))
    mixed_rows = mixed_rows / jnp.transpose(row_total, (2, 0, 1))[..., None]
    return mixed_rows.astype(jnp.bfloat16)

def reference(query_states, key_states, value_states, vertical_blocks, slash_offsets):
    groups = QH // KVH
    query_blocks = query_states.reshape(QB, BS, KVH, groups, HD)
    key_blocks = key_states.reshape(QB, BS, KVH, HD)
    value_blocks = value_states.reshape(QB, BS, KVH, HD)
    head_rows = jnp.arange(KVH, dtype=jnp.int32)[:, None]
    score_scale = 1.0 / math.sqrt(HD)

    def one_block(query_block):
        nearby = jnp.clip(query_block - slash_offsets, 0, QB - 1).astype(jnp.int32)
        key_rows = jnp.concatenate([key_blocks[nearby, :, head_rows, :], key_blocks[vertical_blocks, :, head_rows, :]], axis=1)
        value_rows = jnp.concatenate([value_blocks[nearby, :, head_rows, :], value_blocks[vertical_blocks, :, head_rows, :]], axis=1)
        key_rows = key_rows.reshape(KVH, -1, HD)
        value_rows = value_rows.reshape(KVH, -1, HD)
        active = block_mask(query_block, slash_offsets, vertical_blocks)
        return attend_block(query_blocks[query_block], key_rows, value_rows, active, score_scale)

    def block_group(block_ids):
        return jax.vmap(one_block)(block_ids)
    block_ids = jnp.arange(QB, dtype=jnp.int32).reshape(-1, TOK_DEV // BS)
    mixed_rows = lax.map(block_group, block_ids)
    return mixed_rows.reshape(S, QH * HD)
```

```python
import functools
import math

import jax
import jax.numpy as jnp
from jax import lax
from jax.experimental import pallas as pl
from jax.experimental.pallas import tpu as pltpu
from jax.sharding import PartitionSpec as P

BS = 64
SPAN = 8
MASKED = -1e30


def passed_along(block, axis, distance):
    devices = range(lax.axis_size(axis))
    route = [(i - distance, i) for i in devices if i - distance in devices]
    return lax.ppermute(block, axis, route)


def owned_columns(key_here, value_here, vertical_here, first_block):
    block_count = key_here.shape[0] // BS
    kv_heads = vertical_here.shape[0]
    head_dim = key_here.shape[1] // kv_heads
    key_blocks = key_here.reshape(block_count, BS, kv_heads, head_dim)
    value_blocks = value_here.reshape(block_count, BS, kv_heads, head_dim)
    offset = vertical_here - first_block
    inside = ((offset >= 0) & (offset < block_count))[:, :, None, None]
    picked = jnp.clip(offset, 0, block_count - 1)
    head_rows = jnp.arange(kv_heads, dtype=jnp.int32)[:, None]
    zero_fill = jnp.zeros((), key_here.dtype)
    key_cols = jnp.where(inside, key_blocks[picked, :, head_rows, :], zero_fill)
    value_cols = jnp.where(inside, value_blocks[picked, :, head_rows, :], zero_fill)
    return (key_cols, value_cols)


def attention_kernel(
    vertical, slash, q_ref, nk_ref, nv_ref, wk_ref, wv_ref, o_ref, kbuf, vbuf, causal
):
    g = pl.program_id(0)
    position = lax.axis_index(("seq", "head"))
    tokens = q_ref.shape[0]
    head_dim = nk_ref.shape[1]
    groups = q_ref.shape[1] // head_dim
    block_count = tokens // BS
    window_blocks = nk_ref.shape[0] // BS
    back_blocks = window_blocks - block_count
    ns, nv = slash.shape[1], vertical.shape[1]
    window_first = position * block_count - back_blocks
    scale = math.log2(math.e) / math.sqrt(head_dim)

    @pl.when(g == 0)
    def _():
        row = lax.broadcasted_iota(jnp.int32, causal.shape, 0)
        col = lax.broadcasted_iota(jnp.int32, causal.shape, 1)
        causal[...] = jnp.where((col < BS) & (col > row), MASKED, 0.0)
        vbuf[...] = jnp.ones_like(vbuf)

    offsets = [slash[g, m] for m in range(ns)]
    columns = [vertical[g, m] for m in range(nv)]
    ordered = [jnp.int32(0)] + [
        jnp.where(offsets[m] == 0, offsets[0], offsets[m]) for m in range(1, ns)
    ]
    lane = lax.broadcasted_iota(jnp.int32, (1, (ns + nv) * BS), 1)
    for b in range(block_count):
        query_block = position * block_count + b
        own = back_blocks + b
        bias = jnp.zeros(lane.shape, jnp.float32)
        for m in range(ns + nv):
            rows = pl.ds(m * BS, BS)
            if m < ns:
                active = ordered[m] <= query_block
                at = jnp.where(active, own - ordered[m], own)
                at = pl.multiple_of(at * BS, BS)
                key_block = nk_ref[pl.ds(at, BS), :]
                value_block = nv_ref[pl.ds(at, BS), :]
            else:
                j = columns[m - ns]
                active = j <= query_block
                for off in offsets:
                    active = active & (query_block - j != off)
                near = jnp.logical_not(active) | (j >= window_first)
                at = jnp.where(active & near, j - window_first, own)
                at = pl.multiple_of(at * BS, BS)
                far_rows = pl.ds((m - ns) * BS, BS)
                key_block = jnp.where(near, nk_ref[pl.ds(at, BS), :], wk_ref[0, far_rows, :])
                value_block = jnp.where(near, nv_ref[pl.ds(at, BS), :], wv_ref[0, far_rows, :])
            kbuf[b, rows, :] = key_block
            vbuf[b, rows, :head_dim] = value_block
            here = (lane >= m * BS) & (lane < (m + 1) * BS)
            bias = jnp.where(here, jnp.where(active, 0.0, MASKED), bias)
        q_rows = slice(b * BS, (b + 1) * BS)
        query = jnp.concatenate(
            [q_ref[q_rows, c * head_dim : (c + 1) * head_dim] for c in range(groups)], axis=0
        )
        scores = lax.dot_general(
            query, kbuf[b], (((1,), (1,)), ((), ())), preferred_element_type=jnp.float32
        )
        scores = scores * scale + bias
        edge = causal.shape[1]
        edge_mask = jnp.concatenate([causal[...]] * groups, axis=0)
        scores = jnp.concatenate([scores[:, :edge] + edge_mask, scores[:, edge:]], axis=1)
        row_max = jnp.max(scores, axis=-1, keepdims=True)
        weights = jnp.exp2(scores - row_max).astype(jnp.bfloat16)
        mixed = jnp.dot(weights, vbuf[b], preferred_element_type=jnp.float32)
        mixed = (mixed[:, :head_dim] / mixed[:, head_dim:]).astype(o_ref.dtype)
        for c in range(groups):
            o_ref[q_rows, c * head_dim : (c + 1) * head_dim] = mixed[c * BS : (c + 1) * BS]


def attend(query_here, near_keys, near_values, far_keys, far_values, vertical_here, slash_here):
    length, width = query_here.shape
    kv_heads, nv = vertical_here.shape
    ns = slash_here.shape[1]
    head_dim = near_keys.shape[1] // kv_heads
    group_width = width // kv_heads
    block_count = length // BS
    near_spec = pl.BlockSpec((near_keys.shape[0], head_dim), lambda g, *_: (0, g))
    far_spec = pl.BlockSpec((1, nv * BS, head_dim), lambda g, *_: (g, 0, 0))
    row_spec = pl.BlockSpec((length, group_width), lambda g, *_: (0, g))
    slots = (ns + nv) * BS
    return pl.pallas_call(
        attention_kernel,
        grid_spec=pltpu.PrefetchScalarGridSpec(
            num_scalar_prefetch=2,
            grid=(kv_heads,),
            in_specs=[row_spec, near_spec, near_spec, far_spec, far_spec],
            out_specs=row_spec,
            scratch_shapes=[
                pltpu.VMEM((block_count, slots, head_dim), jnp.bfloat16),
                pltpu.VMEM((block_count, slots, 2 * head_dim), jnp.bfloat16),
                pltpu.VMEM((BS, 128), jnp.float32),
            ],
        ),
        out_shape=jax.ShapeDtypeStruct((length, width), query_here.dtype),
        compiler_params=pltpu.CompilerParams(
            dimension_semantics=("arbitrary",), vmem_limit_bytes=40 * 1024 * 1024
        ),
        cost_estimate=pl.CostEstimate(
            flops=4 * length * width * slots,
            bytes_accessed=4 * length * width,
            transcendentals=length * width // head_dim * slots,
        ),
    )(vertical_here, slash_here, query_here, near_keys, near_values, far_keys, far_values)


def on_device(query_states, key_states, value_states, vertical_blocks, slash_offsets):
    position = lax.axis_index(("seq", "head"))
    length = query_states.shape[0]
    block_count = length // BS
    kv_heads, nv = vertical_blocks.shape
    head_dim = key_states.shape[1] // kv_heads
    back_count = -(-((SPAN - 1) * BS) // length)
    near_keys = [key_states]
    near_values = [value_states]
    for distance in range(1, back_count + 1):
        far_key, far_value = passed_along((key_states, value_states), ("seq", "head"), distance)
        near_keys.insert(0, far_key)
        near_values.insert(0, far_value)
    own_keys, own_values = owned_columns(
        key_states, value_states, vertical_blocks, position * block_count
    )
    summed_keys, summed_values = lax.psum((own_keys, own_values), ("seq", "head"))
    return attend(
        query_states,
        jnp.concatenate(near_keys, axis=0),
        jnp.concatenate(near_values, axis=0),
        summed_keys.reshape(kv_heads, nv * BS, head_dim),
        summed_values.reshape(kv_heads, nv * BS, head_dim),
        vertical_blocks,
        slash_offsets,
    )


def solution(mesh):
    in_specs = (
        P(("parts", "seq", "head"), None),
        P(("parts", "seq", "head"), None),
        P(("parts", "seq", "head"), None),
        P("parts", None),
        P("parts", None),
    )
    out_specs = P(("parts", "seq", "head"), None)
    return jax.shard_map(
        on_device, mesh=mesh, in_specs=in_specs, out_specs=out_specs, check_vma=False
    )
```

```python
import functools
import math

import jax
import jax.numpy as jnp
from jax import lax
from jax.experimental import pallas as pl
from jax.experimental.pallas import tpu as pltpu
from jax.sharding import PartitionSpec as P

BS = 64
SPAN = 8
MASKED = -1e30


MESH = pl.DeviceIdType.MESH


def gather_kernel(
    lanes, k_ref, v_ref, vertical, nk_ref, nv_ref, wk_ref, wv_ref, parts_k, parts_v, merged, send, recv
):
    cores = lax.axis_size("head")
    levels = lax.axis_size("seq") * cores // lanes
    me = lax.axis_index(("seq", "head"))
    level, lane = me // lanes, me % lanes
    side, core = lane // cores, lane % cores
    blocks = k_ref.shape[0]
    share = wk_ref.shape[0] // lanes
    head_dim = wk_ref.shape[2]
    nv = vertical.shape[1]
    across, beside = me + cores * (1 - 2 * side), me + 1 - 2 * core
    above, below = me + lanes, me - lanes
    has_above, has_below = level < levels - 1, level > 0
    always = level >= 0

    def name(device):
        return {"seq": device // cores, "head": device % cores}

    peers = []
    for hop in range(1, lanes):
        peers.append((always, level * lanes + (lane + hop) % lanes))
    peers += [(has_above, above), (has_below, below)]
    barrier = pltpu.get_barrier_semaphore()
    for there, peer in peers:

        @pl.when(there)
        def _():
            pl.semaphore_signal(barrier, inc=1, device_id=name(peer), device_id_type=MESH)

    ends = jnp.where(has_above, 1, 0) + jnp.where(has_below, 1, 0)
    pl.semaphore_wait(barrier, lanes - 1 + ends)

    near = (nk_ref, nv_ref)
    own = (k_ref, v_ref)
    far = (wk_ref, wv_ref)
    parts = (parts_k, parts_v)
    count = [0]

    class Link:
        def __init__(self, sends, gets, source, target, device):
            at = count[0]
            count[0] += 1
            self.sends, self.gets = sends, gets
            self.copy = pltpu.make_async_remote_copy(
                src_ref=source,
                dst_ref=target,
                send_sem=send.at[at],
                recv_sem=recv.at[at],
                device_id=name(device),
                device_id_type=MESH,
            )

        def start(self):
            pl.when(self.sends)(lambda: self.copy.start())

        def arrived(self):
            pl.when(self.gets)(lambda: self.copy.wait_recv())

        def sent(self):
            pl.when(self.sends)(lambda: self.copy.wait_send())

    def slot(ref, distance):
        first = (lanes - distance) * blocks
        return ref.at[first : first + blocks]

    width = share * head_dim
    links = []

    def link(*args):
        links.append(Link(*args))
        return links[-1]

    split, up, out_own, out_far, pair_own, pair_far, pass_low, pass_high = ([] for _ in range(8))
    mine = pl.ds(lane * blocks, blocks)
    crossed = (side == 1) | has_below
    for kv in range(2):
        for hop in range(1, lanes):
            to = (lane + hop) % lanes
            columns = pl.ds(pl.multiple_of(to * width, width), width)
            split.append(
                link(
                    always,
                    always,
                    own[kv].at[:, :, columns],
                    parts[kv].at[mine],
                    level * lanes + to,
                )
            )
        old = slot(near[kv], lanes)
        middle = slot(near[kv], cores)
        first, third = slot(near[kv], 1), slot(near[kv], lanes - 1)
        up.append(link(has_above, has_below, own[kv], old, above))
        out_own.append(link(side == 0, side == 1, own[kv], middle, across))
        out_far.append(
            link((side == 1) & has_below, (side == 0) & has_below, old, middle, across)
        )
        pair_own.append(link(core == 0, core == 1, own[kv], first, beside))
        pair_far.append(link((core == 1) & has_below, (core == 0) & has_below, old, third, beside))
        pass_low.append(link((core == 0) & crossed, (core == 1) & crossed, middle, third, beside))
        pass_high.append(link((core == 1) & crossed, (core == 0) & crossed, middle, first, beside))

    rise, spread_pair, spread_across, spread_last = ([[], []] for _ in range(4))
    opposite = lane + cores * (1 - 2 * side)
    for kv in range(2):
        for h in range(share):
            here = far[kv].at[lane * share + h]
            there = far[kv].at[opposite * share + h]
            rise[kv].append(link(has_above, has_below, merged.at[kv, h], here, above))
            spread_pair[kv].append(link(has_below, has_below, here, here, beside))
            spread_across[kv].append(link(has_below, has_below, here, here, across))
            spread_last[kv].append(link(has_below, has_below, there, there, beside))

    for part in split[: lanes - 1]:
        part.start()
    up[0].start()
    for part in split[lanes - 1 :]:
        part.start()
    for kv in range(2):
        out_own[kv].start()
        pair_own[kv].start()
    my_columns = pl.ds(pl.multiple_of(lane * width, width), width)
    for kv in range(2):
        parts[kv][mine] = own[kv][:, :, my_columns]
        slot(near[kv], 0)[...] = own[kv][...]

    @pl.when(level == 0)
    def _():
        for kv in range(2):
            for h in range(share):
                far[kv][lane * share + h] = jnp.zeros(wk_ref.shape[1:], wk_ref.dtype)

    level_blocks = lanes * blocks
    for kv in range(2):
        for part in split[kv * (lanes - 1) : (kv + 1) * (lanes - 1)]:
            part.arrived()
        up[kv].arrived()
        out_far[kv].start()
        pair_far[kv].start()
        for h in range(share):
            rise[kv][h].arrived()
            spread_across[kv][h].start()
            spread_pair[kv][h].start()
            for m in range(nv):
                at = vertical[lane * share + h, m] - level * level_blocks
                at_all = jnp.full((BS, head_dim), at, jnp.int32)
                inside = (at_all >= 0) & (at_all < level_blocks)
                at = jnp.minimum(jnp.maximum(at, 0), level_blocks - 1)
                rows = slice(m * BS, (m + 1) * BS)
                block = parts[kv][at][:, h * head_dim : (h + 1) * head_dim]
                before = far[kv][lane * share + h, rows, :]
                merged[kv, h, rows, :] = jnp.where(inside, block, before)
            rise[kv][h].start()
        if kv == 0:
            up[1].start()
    for kv in range(2):
        out_own[kv].arrived()
        out_far[kv].arrived()
        pass_low[kv].start()
        pass_high[kv].start()
    for kv in range(2):
        for h in range(share):
            spread_across[kv][h].arrived()
            spread_last[kv][h].start()
    for kv in range(2):
        pair_own[kv].arrived()
        pair_far[kv].arrived()
        pass_low[kv].arrived()
        pass_high[kv].arrived()
        for h in range(share):
            spread_pair[kv][h].arrived()
    for kv in range(2):
        for h in range(share):
            spread_last[kv][h].arrived()
    for each in links:
        each.sent()


def gather(key_here, value_here, vertical_here):
    tokens, width = key_here.shape
    kv_heads, nv = vertical_here.shape
    head_dim = width // kv_heads
    lanes = -(-((SPAN - 1) * BS) // tokens)
    share = kv_heads // lanes
    vmem = pl.BlockSpec(memory_space=pltpu.VMEM)
    blocks = tokens // BS
    near = jax.ShapeDtypeStruct(((lanes + 1) * blocks, BS, width), key_here.dtype)
    far = jax.ShapeDtypeStruct((kv_heads, nv * BS, head_dim), key_here.dtype)
    copies = 2 * (lanes - 1 + 7 + 4 * share)
    near_keys, near_values, far_keys, far_values = pl.pallas_call(
        functools.partial(gather_kernel, lanes),
        in_specs=[vmem, vmem, pl.BlockSpec(memory_space=pltpu.SMEM)],
        out_specs=[vmem] * 4,
        out_shape=[near, near, far, far],
        scratch_shapes=[
            pltpu.VMEM((lanes * blocks, BS, share * head_dim), key_here.dtype),
            pltpu.VMEM((lanes * blocks, BS, share * head_dim), key_here.dtype),
            pltpu.VMEM((2, share, nv * BS, head_dim), key_here.dtype),
            pltpu.SemaphoreType.DMA((copies,)),
            pltpu.SemaphoreType.DMA((copies,)),
        ],
        compiler_params=pltpu.CompilerParams(
            collective_id=0, has_side_effects=True, vmem_limit_bytes=40 * 1024 * 1024
        ),
    )(
        key_here.reshape(blocks, BS, width), value_here.reshape(blocks, BS, width), vertical_here
    )
    return near_keys.reshape(-1, width), near_values.reshape(-1, width), far_keys, far_values


def attention_kernel(
    vertical, slash, q_ref, nk_ref, nv_ref, wk_ref, wv_ref, o_ref, kbuf, vbuf, causal
):
    g = pl.program_id(0)
    position = lax.axis_index(("seq", "head"))
    tokens = q_ref.shape[0]
    head_dim = nk_ref.shape[1]
    groups = q_ref.shape[1] // head_dim
    block_count = tokens // BS
    window_blocks = nk_ref.shape[0] // BS
    back_blocks = window_blocks - block_count
    ns, nv = slash.shape[1], vertical.shape[1]
    window_first = position * block_count - back_blocks
    scale = math.log2(math.e) / math.sqrt(head_dim)

    @pl.when(g == 0)
    def _():
        row = lax.broadcasted_iota(jnp.int32, causal.shape, 0)
        col = lax.broadcasted_iota(jnp.int32, causal.shape, 1)
        causal[...] = jnp.where((col < BS) & (col > row), MASKED, 0.0)
        vbuf[...] = jnp.ones_like(vbuf)

    offsets = [slash[g, m] for m in range(ns)]
    columns = [vertical[g, m] for m in range(nv)]
    ordered = [jnp.int32(0)] + [
        jnp.where(offsets[m] == 0, offsets[0], offsets[m]) for m in range(1, ns)
    ]
    lane = lax.broadcasted_iota(jnp.int32, (1, (ns + nv) * BS), 1)
    for b in range(block_count):
        query_block = position * block_count + b
        own = back_blocks + b
        bias = jnp.zeros(lane.shape, jnp.float32)
        for m in range(ns + nv):
            rows = pl.ds(m * BS, BS)
            if m < ns:
                active = ordered[m] <= query_block
                at = jnp.where(active, own - ordered[m], own)
                at = pl.multiple_of(at * BS, BS)
                key_block = nk_ref[pl.ds(at, BS), :]
                value_block = nv_ref[pl.ds(at, BS), :]
            else:
                j = columns[m - ns]
                active = j <= query_block
                for off in offsets:
                    active = active & (query_block - j != off)
                near = jnp.logical_not(active) | (j >= window_first)
                at = jnp.where(active & near, j - window_first, own)
                at = pl.multiple_of(at * BS, BS)
                far_rows = pl.ds((m - ns) * BS, BS)
                key_block = jnp.where(near, nk_ref[pl.ds(at, BS), :], wk_ref[0, far_rows, :])
                value_block = jnp.where(near, nv_ref[pl.ds(at, BS), :], wv_ref[0, far_rows, :])
            kbuf[b, rows, :] = key_block
            vbuf[b, rows, :head_dim] = value_block
            here = (lane >= m * BS) & (lane < (m + 1) * BS)
            bias = jnp.where(here, jnp.where(active, 0.0, MASKED), bias)
        q_rows = slice(b * BS, (b + 1) * BS)
        query = jnp.concatenate(
            [q_ref[q_rows, c * head_dim : (c + 1) * head_dim] for c in range(groups)], axis=0
        )
        scores = lax.dot_general(
            query, kbuf[b], (((1,), (1,)), ((), ())), preferred_element_type=jnp.float32
        )
        scores = scores * scale + bias
        edge = causal.shape[1]
        edge_mask = jnp.concatenate([causal[...]] * groups, axis=0)
        scores = jnp.concatenate([scores[:, :edge] + edge_mask, scores[:, edge:]], axis=1)
        row_max = jnp.max(scores, axis=-1, keepdims=True)
        weights = jnp.exp2(scores - row_max).astype(jnp.bfloat16)
        mixed = jnp.dot(weights, vbuf[b], preferred_element_type=jnp.float32)
        mixed = (mixed[:, :head_dim] / mixed[:, head_dim:]).astype(o_ref.dtype)
        for c in range(groups):
            o_ref[q_rows, c * head_dim : (c + 1) * head_dim] = mixed[c * BS : (c + 1) * BS]


def attend(query_here, near_keys, near_values, far_keys, far_values, vertical_here, slash_here):
    length, width = query_here.shape
    kv_heads, nv = vertical_here.shape
    ns = slash_here.shape[1]
    head_dim = near_keys.shape[1] // kv_heads
    group_width = width // kv_heads
    block_count = length // BS
    near_spec = pl.BlockSpec((near_keys.shape[0], head_dim), lambda g, *_: (0, g))
    far_spec = pl.BlockSpec((1, nv * BS, head_dim), lambda g, *_: (g, 0, 0))
    row_spec = pl.BlockSpec((length, group_width), lambda g, *_: (0, g))
    slots = (ns + nv) * BS
    return pl.pallas_call(
        attention_kernel,
        grid_spec=pltpu.PrefetchScalarGridSpec(
            num_scalar_prefetch=2,
            grid=(kv_heads,),
            in_specs=[row_spec, near_spec, near_spec, far_spec, far_spec],
            out_specs=row_spec,
            scratch_shapes=[
                pltpu.VMEM((block_count, slots, head_dim), jnp.bfloat16),
                pltpu.VMEM((block_count, slots, 2 * head_dim), jnp.bfloat16),
                pltpu.VMEM((BS, 128), jnp.float32),
            ],
        ),
        out_shape=jax.ShapeDtypeStruct((length, width), query_here.dtype),
        compiler_params=pltpu.CompilerParams(
            dimension_semantics=("arbitrary",), vmem_limit_bytes=40 * 1024 * 1024
        ),
        cost_estimate=pl.CostEstimate(
            flops=4 * length * width * slots,
            bytes_accessed=4 * length * width,
            transcendentals=length * width // head_dim * slots,
        ),
    )(vertical_here, slash_here, query_here, near_keys, near_values, far_keys, far_values)


def on_device(query_states, key_states, value_states, vertical_blocks, slash_offsets):
    gathered = gather(key_states, value_states, vertical_blocks)
    return attend(query_states, *gathered, vertical_blocks, slash_offsets)


def solution(mesh):
    in_specs = (
        P(("parts", "seq", "head"), None),
        P(("parts", "seq", "head"), None),
        P(("parts", "seq", "head"), None),
        P("parts", None),
        P("parts", None),
    )
    out_specs = P(("parts", "seq", "head"), None)
    return jax.shard_map(
        on_device, mesh=mesh, in_specs=in_specs, out_specs=out_specs, check_vma=False
    )
```

```python
import functools
import math

import jax
import jax.numpy as jnp
from jax import lax
from jax.experimental import pallas as pl
from jax.experimental.pallas import tpu as pltpu
from jax.sharding import PartitionSpec as P

BS = 64
SPAN = 8
MASKED = -1e30


MESH = pl.DeviceIdType.MESH


def gather_kernel(
    lanes, k_ref, v_ref, vertical, nk_ref, nv_ref, wk_ref, wv_ref, parts_k, parts_v, merged, send, recv
):
    cores = lax.axis_size("head")
    levels = lax.axis_size("seq") * cores // lanes
    me = lax.axis_index(("seq", "head"))
    level, lane = me // lanes, me % lanes
    side, core = lane // cores, lane % cores
    blocks = k_ref.shape[0]
    share = wk_ref.shape[0] // lanes
    head_dim = wk_ref.shape[2]
    nv = vertical.shape[1]
    across, beside = me + cores * (1 - 2 * side), me + 1 - 2 * core
    above, below = me + lanes, me - lanes
    has_above, has_below = level < levels - 1, level > 0
    always = level >= 0

    def name(device):
        return {"seq": device // cores, "head": device % cores}

    peers = []
    for hop in range(1, lanes):
        peers.append((always, level * lanes + (lane + hop) % lanes))
    peers += [(has_above, above), (has_below, below)]
    barrier = pltpu.get_barrier_semaphore()
    for there, peer in peers:

        @pl.when(there)
        def _():
            pl.semaphore_signal(barrier, inc=1, device_id=name(peer), device_id_type=MESH)

    ends = jnp.where(has_above, 1, 0) + jnp.where(has_below, 1, 0)
    pl.semaphore_wait(barrier, lanes - 1 + ends)

    near = (nk_ref, nv_ref)
    own = (k_ref, v_ref)
    far = (wk_ref, wv_ref)
    parts = (parts_k, parts_v)
    count = [0]

    class Link:
        def __init__(self, sends, gets, source, target, device):
            at = count[0]
            count[0] += 1
            self.sends, self.gets = sends, gets
            self.copy = pltpu.make_async_remote_copy(
                src_ref=source,
                dst_ref=target,
                send_sem=send.at[at],
                recv_sem=recv.at[at],
                device_id=name(device),
                device_id_type=MESH,
            )

        def start(self, when=True):
            pl.when(self.sends & when)(lambda: self.copy.start())

        def arrived(self, when=True):
            pl.when(self.gets & when)(lambda: self.copy.wait_recv())

        def sent(self):
            pl.when(self.sends)(lambda: self.copy.wait_send())

    def slot(ref, distance):
        first = (lanes - distance) * blocks
        return ref.at[first : first + blocks]

    width = share * head_dim
    links = []

    def link(*args):
        links.append(Link(*args))
        return links[-1]

    split, up, out_own, out_far, pair_own, pair_far, pass_low, pass_high = ([] for _ in range(8))
    mine = pl.ds(lane * blocks, blocks)
    crossed = (side == 1) | has_below
    for kv in range(2):
        for hop in range(1, lanes):
            to = (lane + hop) % lanes
            columns = pl.ds(pl.multiple_of(to * width, width), width)
            split.append(
                link(
                    always,
                    always,
                    own[kv].at[:, :, columns],
                    parts[kv].at[mine],
                    level * lanes + to,
                )
            )
        old = slot(near[kv], lanes)
        middle = slot(near[kv], cores)
        first, third = slot(near[kv], 1), slot(near[kv], lanes - 1)
        up.append(link(has_above, has_below, own[kv], old, above))
        out_own.append(link(side == 0, side == 1, own[kv], middle, across))
        out_far.append(
            link((side == 1) & has_below, (side == 0) & has_below, old, middle, across)
        )
        pair_own.append(link(core == 0, core == 1, own[kv], first, beside))
        pair_far.append(link((core == 1) & has_below, (core == 0) & has_below, old, third, beside))
        pass_low.append(link((core == 0) & crossed, (core == 1) & crossed, middle, third, beside))
        pass_high.append(link((core == 1) & crossed, (core == 0) & crossed, middle, first, beside))

    rise, spread_pair, spread_across, spread_last = ([[], []] for _ in range(4))
    opposite = lane + cores * (1 - 2 * side)
    for kv in range(2):
        for h in range(share):
            here = far[kv].at[lane * share + h]
            there = far[kv].at[opposite * share + h]
            rise[kv].append(link(has_above, has_below, merged.at[kv, h], here, above))
            spread_pair[kv].append(link(has_below, has_below, here, here, beside))
            spread_across[kv].append(link(has_below, has_below, here, here, across))
            spread_last[kv].append(link(has_below, has_below, there, there, beside))

    for part in split[: lanes - 1]:
        part.start()
    up[0].start()
    for part in split[lanes - 1 :]:
        part.start()
    up[1].start(has_below)
    for kv in range(2):
        out_own[kv].start()
        pair_own[kv].start()
    my_columns = pl.ds(pl.multiple_of(lane * width, width), width)
    for kv in range(2):
        parts[kv][mine] = own[kv][:, :, my_columns]
        slot(near[kv], 0)[...] = own[kv][...]

    @pl.when(level == 0)
    def _():
        for kv in range(2):
            for h in range(share):
                far[kv][lane * share + h] = jnp.zeros(wk_ref.shape[1:], wk_ref.dtype)

    level_blocks = lanes * blocks
    def pass_on(kv, when=True):
        up[kv].arrived(when)
        out_far[kv].start(when)
        pair_far[kv].start(when)

    for part in split[: lanes - 1]:
        part.arrived()
    pass_on(0)
    pass_on(1, level > 1)
    for kv in range(2):
        if kv == 1:
            for part in split[lanes - 1 :]:
                part.arrived()
        for h in range(share):
            rise[kv][h].arrived()
            for m in range(nv):
                at = vertical[lane * share + h, m] - level * level_blocks
                at_all = jnp.full((BS, head_dim), at, jnp.int32)
                inside = (at_all >= 0) & (at_all < level_blocks)
                at = jnp.minimum(jnp.maximum(at, 0), level_blocks - 1)
                rows = slice(m * BS, (m + 1) * BS)
                block = parts[kv][at][:, h * head_dim : (h + 1) * head_dim]
                before = far[kv][lane * share + h, rows, :]
                merged[kv, h, rows, :] = jnp.where(inside, block, before)
            rise[kv][h].start()
            spread_across[kv][h].start()
            spread_pair[kv][h].start()
    up[1].start(level == 0)
    pass_on(1, level == 1)
    for kv in range(2):
        out_own[kv].arrived()
        out_far[kv].arrived()
        pass_low[kv].start()
        pass_high[kv].start()
    for kv in range(2):
        for h in range(share):
            spread_across[kv][h].arrived()
            spread_last[kv][h].start()
    for kv in range(2):
        pair_own[kv].arrived()
        pair_far[kv].arrived()
        pass_low[kv].arrived()
        pass_high[kv].arrived()
        for h in range(share):
            spread_pair[kv][h].arrived()
    for kv in range(2):
        for h in range(share):
            spread_last[kv][h].arrived()
    for each in links:
        each.sent()


def gather(key_here, value_here, vertical_here):
    tokens, width = key_here.shape
    kv_heads, nv = vertical_here.shape
    head_dim = width // kv_heads
    lanes = -(-((SPAN - 1) * BS) // tokens)
    share = kv_heads // lanes
    vmem = pl.BlockSpec(memory_space=pltpu.VMEM)
    blocks = tokens // BS
    near = jax.ShapeDtypeStruct(((lanes + 1) * blocks, BS, width), key_here.dtype)
    far = jax.ShapeDtypeStruct((kv_heads, nv * BS, head_dim), key_here.dtype)
    copies = 2 * (lanes - 1 + 7 + 4 * share)
    near_keys, near_values, far_keys, far_values = pl.pallas_call(
        functools.partial(gather_kernel, lanes),
        in_specs=[vmem, vmem, pl.BlockSpec(memory_space=pltpu.SMEM)],
        out_specs=[vmem] * 4,
        out_shape=[near, near, far, far],
        scratch_shapes=[
            pltpu.VMEM((lanes * blocks, BS, share * head_dim), key_here.dtype),
            pltpu.VMEM((lanes * blocks, BS, share * head_dim), key_here.dtype),
            pltpu.VMEM((2, share, nv * BS, head_dim), key_here.dtype),
            pltpu.SemaphoreType.DMA((copies,)),
            pltpu.SemaphoreType.DMA((copies,)),
        ],
        compiler_params=pltpu.CompilerParams(
            collective_id=0, has_side_effects=True, vmem_limit_bytes=16 * 1024 * 1024
        ),
    )(
        key_here.reshape(blocks, BS, width), value_here.reshape(blocks, BS, width), vertical_here
    )
    return near_keys.reshape(-1, width), near_values.reshape(-1, width), far_keys, far_values


def attention_kernel(
    vertical, slash, q_ref, nk_ref, nv_ref, wk_ref, wv_ref, o_ref, kbuf, vbuf
):
    g = pl.program_id(0)
    position = lax.axis_index(("seq", "head"))
    tokens = q_ref.shape[0]
    head_dim = nk_ref.shape[1]
    groups = q_ref.shape[1] // head_dim
    block_count = tokens // BS
    window_blocks = nk_ref.shape[0] // BS
    back_blocks = window_blocks - block_count
    ns, nv = slash.shape[1], vertical.shape[1]
    window_first = position * block_count - back_blocks
    scale = math.log2(math.e) / math.sqrt(head_dim)

    row = lax.broadcasted_iota(jnp.int32, (BS, head_dim), 0)
    col = lax.broadcasted_iota(jnp.int32, (BS, head_dim), 1)
    token = jnp.where(row == col, 1.0, 0.0).astype(kbuf.dtype)

    @pl.when(g == 0)
    def _():
        vbuf[...] = jnp.ones_like(vbuf)
        later = jnp.where((col < BS) & (row > col), MASKED, 0.0).astype(kbuf.dtype)
        for b in range(block_count):
            kbuf[b, :BS, head_dim:] = later

    offsets = [slash[g, m] for m in range(ns)]
    columns = [vertical[g, m] for m in range(nv)]
    ordered = [jnp.int32(0)] + [
        jnp.where(offsets[m] == 0, offsets[0], offsets[m]) for m in range(1, ns)
    ]
    for b in range(block_count):
        query_block = position * block_count + b
        own = back_blocks + b
        for m in range(ns + nv):
            rows = pl.ds(m * BS, BS)
            if m < ns:
                active = ordered[m] <= query_block
                at = jnp.where(active, own - ordered[m], own)
                at = pl.multiple_of(at * BS, BS)
                key_block = nk_ref[pl.ds(at, BS), :]
                value_block = nv_ref[pl.ds(at, BS), :]
            else:
                j = columns[m - ns]
                active = j <= query_block
                for off in offsets:
                    active = active & (query_block - j != off)
                near = jnp.logical_not(active) | (j >= window_first)
                at = jnp.where(active & near, j - window_first, own)
                at = pl.multiple_of(at * BS, BS)
                far_rows = pl.ds((m - ns) * BS, BS)
                key_block = jnp.where(near, nk_ref[pl.ds(at, BS), :], wk_ref[0, far_rows, :])
                value_block = jnp.where(near, nv_ref[pl.ds(at, BS), :], wv_ref[0, far_rows, :])
            kbuf[b, rows, :head_dim] = key_block
            vbuf[b, rows, :head_dim] = value_block
            if m > 0:
                hidden = jnp.full((BS, head_dim), jnp.where(active, 0.0, MASKED), jnp.float32)
                kbuf[b, rows, head_dim:] = hidden.astype(kbuf.dtype)
        q_rows = slice(b * BS, (b + 1) * BS)
        query = jnp.concatenate(
            [
                jnp.concatenate([q_ref[q_rows, c * head_dim : (c + 1) * head_dim], token], axis=1)
                for c in range(groups)
            ],
            axis=0,
        )
        scores = lax.dot_general(
            query, kbuf[b], (((1,), (1,)), ((), ())), preferred_element_type=jnp.float32
        )
        row_max = jnp.max(scores, axis=-1, keepdims=True)
        weights = jnp.exp2((scores - row_max) * scale).astype(jnp.bfloat16)
        mixed = jnp.dot(weights, vbuf[b], preferred_element_type=jnp.float32)
        mixed = (mixed[:, :head_dim] / mixed[:, head_dim:]).astype(o_ref.dtype)
        for c in range(groups):
            o_ref[q_rows, c * head_dim : (c + 1) * head_dim] = mixed[c * BS : (c + 1) * BS]


def attend(query_here, near_keys, near_values, far_keys, far_values, vertical_here, slash_here):
    length, width = query_here.shape
    kv_heads, nv = vertical_here.shape
    ns = slash_here.shape[1]
    head_dim = near_keys.shape[1] // kv_heads
    group_width = width // kv_heads
    block_count = length // BS
    near_spec = pl.BlockSpec((near_keys.shape[0], head_dim), lambda g, *_: (0, g))
    far_spec = pl.BlockSpec((1, nv * BS, head_dim), lambda g, *_: (g, 0, 0))
    row_spec = pl.BlockSpec((length, group_width), lambda g, *_: (0, g))
    slots = (ns + nv) * BS
    return pl.pallas_call(
        attention_kernel,
        grid_spec=pltpu.PrefetchScalarGridSpec(
            num_scalar_prefetch=2,
            grid=(kv_heads,),
            in_specs=[row_spec, near_spec, near_spec, far_spec, far_spec],
            out_specs=row_spec,
            scratch_shapes=[
                pltpu.VMEM((block_count, slots, 2 * head_dim), jnp.bfloat16),
                pltpu.VMEM((block_count, slots, 2 * head_dim), jnp.bfloat16),
            ],
        ),
        out_shape=jax.ShapeDtypeStruct((length, width), query_here.dtype),
        compiler_params=pltpu.CompilerParams(
            dimension_semantics=("arbitrary",), vmem_limit_bytes=24 * 1024 * 1024
        ),
        cost_estimate=pl.CostEstimate(
            flops=4 * length * width * slots,
            bytes_accessed=4 * length * width,
            transcendentals=length * width // head_dim * slots,
        ),
    )(vertical_here, slash_here, query_here, near_keys, near_values, far_keys, far_values)


def on_device(query_states, key_states, value_states, vertical_blocks, slash_offsets):
    gathered = gather(key_states, value_states, vertical_blocks)
    return attend(query_states, *gathered, vertical_blocks, slash_offsets)


def solution(mesh):
    in_specs = (
        P(("parts", "seq", "head"), None),
        P(("parts", "seq", "head"), None),
        P(("parts", "seq", "head"), None),
        P("parts", None),
        P("parts", None),
    )
    out_specs = P(("parts", "seq", "head"), None)
    return jax.shard_map(
        on_device, mesh=mesh, in_specs=in_specs, out_specs=out_specs, check_vma=False
    )
```

```python
import functools
import math

import jax
import jax.numpy as jnp
from jax import lax
from jax.experimental import pallas as pl
from jax.experimental.pallas import tpu as pltpu
from jax.sharding import PartitionSpec as P

BS = 64
SPAN = 8
MASKED = -1e30


MESH = pl.DeviceIdType.MESH


def fused_kernel(
    lanes,
    q_hbm,
    k_ref,
    v_ref,
    vertical,
    slash,
    o_ref,
    q_ref,
    nk_ref,
    nv_ref,
    wk_ref,
    wv_ref,
    parts_k,
    parts_v,
    merged,
    kbuf,
    vbuf,
    top,
    total,
    mixed,
    send,
    recv,
    local,
):
    cores = lax.axis_size("head")
    levels = lax.axis_size("seq") * cores // lanes
    me = lax.axis_index(("seq", "head"))
    level, lane = me // lanes, me % lanes
    side, core = lane // cores, lane % cores
    blocks = k_ref.shape[0]
    share = wk_ref.shape[0] // lanes
    head_dim = wk_ref.shape[2]
    nv = vertical.shape[1]
    across, beside = me + cores * (1 - 2 * side), me + 1 - 2 * core
    above, below = me + lanes, me - lanes
    has_above, has_below = level < levels - 1, level > 0
    always = level >= 0

    def name(device):
        return {"seq": device // cores, "head": device % cores}

    peers = []
    for hop in range(1, lanes):
        peers.append((always, level * lanes + (lane + hop) % lanes))
    peers += [(has_above, above), (has_below, below)]
    barrier = pltpu.get_barrier_semaphore()
    for there, peer in peers:

        @pl.when(there)
        def _():
            pl.semaphore_signal(barrier, inc=1, device_id=name(peer), device_id_type=MESH)

    ends = jnp.where(has_above, 1, 0) + jnp.where(has_below, 1, 0)
    pl.semaphore_wait(barrier, lanes - 1 + ends)

    near = (nk_ref, nv_ref)
    own = (k_ref, v_ref)
    far = (wk_ref, wv_ref)
    parts = (parts_k, parts_v)
    count = [0]

    class Link:
        def __init__(self, sends, gets, source, target, device):
            at = count[0]
            count[0] += 1
            self.sends, self.gets = sends, gets
            self.copy = pltpu.make_async_remote_copy(
                src_ref=source,
                dst_ref=target,
                send_sem=send.at[at],
                recv_sem=recv.at[at],
                device_id=name(device),
                device_id_type=MESH,
            )

        def start(self, when=True):
            pl.when(self.sends & when)(lambda: self.copy.start())

        def arrived(self, when=True):
            pl.when(self.gets & when)(lambda: self.copy.wait_recv())

        def sent(self):
            pl.when(self.sends)(lambda: self.copy.wait_send())

    def slot(ref, distance):
        first = (lanes - distance) * blocks
        return ref.at[first : first + blocks]

    width = share * head_dim
    links = []

    def link(*args):
        links.append(Link(*args))
        return links[-1]

    split, up, out_own, out_far, pair_own, pair_far, pass_low, pass_high = ([] for _ in range(8))
    mine = pl.ds(lane * blocks, blocks)
    crossed = (side == 1) | has_below
    for kv in range(2):
        for hop in range(1, lanes):
            to = (lane + hop) % lanes
            columns = pl.ds(pl.multiple_of(to * width, width), width)
            split.append(
                link(
                    always,
                    always,
                    own[kv].at[:, :, columns],
                    parts[kv].at[mine],
                    level * lanes + to,
                )
            )
        old = slot(near[kv], lanes)
        middle = slot(near[kv], cores)
        first, third = slot(near[kv], 1), slot(near[kv], lanes - 1)
        up.append(link(has_above, has_below, own[kv], old, above))
        out_own.append(link(side == 0, side == 1, own[kv], middle, across))
        out_far.append(
            link((side == 1) & has_below, (side == 0) & has_below, old, middle, across)
        )
        pair_own.append(link(core == 0, core == 1, own[kv], first, beside))
        pair_far.append(link((core == 1) & has_below, (core == 0) & has_below, old, third, beside))
        pass_low.append(link((core == 0) & crossed, (core == 1) & crossed, middle, third, beside))
        pass_high.append(link((core == 1) & crossed, (core == 0) & crossed, middle, first, beside))

    rise, spread_pair, spread_across, spread_last = ([[], []] for _ in range(4))
    opposite = lane + cores * (1 - 2 * side)
    for kv in range(2):
        for h in range(share):
            here = far[kv].at[lane * share + h]
            there = far[kv].at[opposite * share + h]
            rise[kv].append(link(has_above, has_below, merged.at[kv, h], here, above))
            spread_pair[kv].append(link(has_below, has_below, here, here, beside))
            spread_across[kv].append(link(has_below, has_below, here, here, across))
            spread_last[kv].append(link(has_below, has_below, there, there, beside))

    for part in split[: lanes - 1]:
        part.start()
    up[0].start()
    for part in split[lanes - 1 :]:
        part.start()
    up[1].start(has_below)
    for kv in range(2):
        out_own[kv].start()
        pair_own[kv].start()
    my_columns = pl.ds(pl.multiple_of(lane * width, width), width)
    kept = []
    for kv in range(2):
        kept.append((own[kv].at[:, :, my_columns], parts[kv].at[mine]))
        kept.append((own[kv], slot(near[kv], 0)))
    kept.append((q_hbm, q_ref))
    kept = [
        pltpu.make_async_copy(source, target, local.at[i])
        for i, (source, target) in enumerate(kept)
    ]
    for copy in kept:
        copy.start()

    @pl.when(level == 0)
    def _():
        for kv in range(2):
            for h in range(share):
                far[kv][lane * share + h] = jnp.zeros(wk_ref.shape[1:], wk_ref.dtype)

    level_blocks = lanes * blocks
    def pass_on(kv, when=True):
        up[kv].arrived(when)
        out_far[kv].start(when)
        pair_far[kv].start(when)

    for part in split[: lanes - 1]:
        part.arrived()
    for copy in kept:
        copy.wait()
    pass_on(0)
    pass_on(1, level > 1)
    for kv in range(2):
        if kv == 1:
            for part in split[lanes - 1 :]:
                part.arrived()
        for h in range(share):
            rise[kv][h].arrived()
            for m in range(nv):
                at = vertical[lane * share + h, m] - level * level_blocks
                at_all = jnp.full((BS, head_dim), at, jnp.int32)
                inside = (at_all >= 0) & (at_all < level_blocks)
                at = jnp.minimum(jnp.maximum(at, 0), level_blocks - 1)
                rows = slice(m * BS, (m + 1) * BS)
                block = parts[kv][at][:, h * head_dim : (h + 1) * head_dim]
                before = far[kv][lane * share + h, rows, :]
                merged[kv, h, rows, :] = jnp.where(inside, block, before)
            rise[kv][h].start()
            spread_across[kv][h].start()
            spread_pair[kv][h].start()
    up[1].start(level == 0)
    pass_on(1, level == 1)
    for kv in range(2):
        out_own[kv].arrived()
        out_far[kv].arrived()
        pass_low[kv].start()
        pass_high[kv].start()
    for kv in range(2):
        pair_own[kv].arrived()
        pair_far[kv].arrived()
        pass_low[kv].arrived()
        pass_high[kv].arrived()

    ns = slash.shape[1]
    groups = q_ref.shape[1] // (wk_ref.shape[0] * head_dim)
    back = lanes * blocks
    window_first = me * blocks - back
    scale = math.log2(math.e) / math.sqrt(head_dim)
    row = lax.broadcasted_iota(jnp.int32, (BS, head_dim), 0)
    col = lax.broadcasted_iota(jnp.int32, (BS, head_dim), 1)
    token = jnp.where(row == col, 1.0, 0.0).astype(kbuf.dtype)
    later = jnp.where((col < BS) & (row > col), MASKED, 0.0).astype(kbuf.dtype)
    vbuf[...] = jnp.ones_like(vbuf)

    def at_least_zero(number):
        return jnp.minimum(jnp.maximum(number + 1, 0), 1)

    def hide(active):
        shown = jnp.full((BS, head_dim), active, jnp.int32).astype(jnp.float32)
        return ((1.0 - shown) * MASKED).astype(kbuf.dtype)

    def rows_of(b):
        return slice(b * BS, (b + 1) * BS)

    def query_of(g, b):
        tiles = []
        for c in range(groups):
            first = pl.multiple_of((g * groups + c) * head_dim, head_dim)
            tiles.append(
                jnp.concatenate([q_ref[rows_of(b), pl.ds(first, head_dim)], token], axis=1)
            )
        return jnp.concatenate(tiles, axis=0)

    def score(g, b):
        return lax.dot_general(
            query_of(g, b), kbuf[b], (((1,), (1,)), ((), ())), preferred_element_type=jnp.float32
        )

    def attend_slash(g, carry):
        columns = pl.ds(pl.multiple_of(g * head_dim, head_dim), head_dim)
        offsets = [slash[g, m] for m in range(ns)]
        for b in range(blocks):
            for m in range(ns):
                rows = slice(m * BS, (m + 1) * BS)
                if m == 0:
                    at = back + b
                    kbuf[b, rows, head_dim:] = later
                else:
                    is_own = 1 - jnp.minimum(offsets[m], 1)
                    offset = offsets[m] + is_own * offsets[0]
                    active = at_least_zero(me * blocks + b - offset)
                    at = back + b - offset * active
                    kbuf[b, rows, head_dim:] = hide(active)
                kbuf[b, rows, :head_dim] = nk_ref[at, :, columns]
                vbuf[b, rows, :head_dim] = nv_ref[at, :, columns]
        for b in range(blocks):
            scores = score(g, b)
            row_max = jnp.max(scores, axis=-1, keepdims=True)
            weights = jnp.exp2((scores - row_max) * scale).astype(kbuf.dtype)
            both = jnp.dot(weights, vbuf[b], preferred_element_type=jnp.float32)
            mixed[g, b] = both[:, :head_dim]
            total[g, b] = both[:, head_dim:]
            top[g, b] = jnp.broadcast_to(row_max, top.shape[2:])
        return carry

    def attend_vertical(g, carry):
        columns = pl.ds(pl.multiple_of(g * head_dim, head_dim), head_dim)
        offsets = [slash[g, m] for m in range(ns)]
        for b in range(blocks):
            query_block = me * blocks + b
            for m in range(nv):
                rows = slice(m * BS, (m + 1) * BS)
                j = vertical[g, m]
                active = at_least_zero(query_block - j)
                for offset in offsets:
                    gap = query_block - j - offset
                    active = active * jnp.minimum(jnp.maximum(gap, -gap), 1)
                inside = at_least_zero(j - window_first)
                far_here = active * (1 - inside)
                at = back + b + active * inside * (j - window_first - back - b)
                use_far = jnp.full((BS, head_dim), far_here, jnp.int32) > 0
                kbuf[b, rows, head_dim:] = hide(active)
                kbuf[b, rows, :head_dim] = jnp.where(
                    use_far, wk_ref[g, rows, :], nk_ref[at, :, columns]
                )
                vbuf[b, rows, :head_dim] = jnp.where(
                    use_far, wv_ref[g, rows, :], nv_ref[at, :, columns]
                )
        for b in range(blocks):
            scores = score(g, b)
            old_max = top[g, b]
            row_max = jnp.maximum(old_max, jnp.max(scores, axis=-1, keepdims=True))
            keep = jnp.exp2((old_max - row_max) * scale)
            weights = jnp.exp2((scores - row_max[:, :1]) * scale).astype(kbuf.dtype)
            both = jnp.dot(weights, vbuf[b], preferred_element_type=jnp.float32)
            result = (mixed[g, b] * keep + both[:, :head_dim]) / (
                total[g, b] * keep + both[:, head_dim:]
            )
            result = result.astype(o_ref.dtype)
            for c in range(groups):
                first = pl.multiple_of((g * groups + c) * head_dim, head_dim)
                o_ref[rows_of(b), pl.ds(first, head_dim)] = result[rows_of(c)]
        return carry

    heads = wk_ref.shape[0]
    lax.fori_loop(0, heads, attend_slash, 0)
    for kv in range(2):
        for h in range(share):
            spread_across[kv][h].arrived()
            spread_last[kv][h].start()
    for kv in range(2):
        for h in range(share):
            spread_pair[kv][h].arrived()
            spread_last[kv][h].arrived()
    lax.fori_loop(0, heads, attend_vertical, 0)
    for each in links:
        each.sent()


def on_device(query_here, key_here, value_here, vertical_here, slash_here):
    tokens, width = key_here.shape
    kv_heads, nv = vertical_here.shape
    ns = slash_here.shape[1]
    head_dim = width // kv_heads
    groups = query_here.shape[1] // width
    lanes = -(-((SPAN - 1) * BS) // tokens)
    share = kv_heads // lanes
    blocks = tokens // BS
    kind = key_here.dtype
    anywhere = pl.BlockSpec(memory_space=pl.ANY)
    scalars = pl.BlockSpec(memory_space=pltpu.SMEM)
    near = pltpu.VMEM(((lanes + 1) * blocks, BS, width), kind)
    far = pltpu.VMEM((kv_heads, nv * BS, head_dim), kind)
    part = pltpu.VMEM((lanes * blocks, BS, share * head_dim), kind)
    slots = max(ns, nv) * BS
    operand = pltpu.VMEM((blocks, slots, 2 * head_dim), kind)
    state = pltpu.VMEM((kv_heads, blocks, groups * BS, head_dim), jnp.float32)
    copies = 2 * (lanes - 1 + 7 + 4 * share)
    return pl.pallas_call(
        functools.partial(fused_kernel, lanes),
        in_specs=[anywhere, anywhere, anywhere, scalars, scalars],
        out_specs=pl.BlockSpec(memory_space=pltpu.VMEM),
        out_shape=jax.ShapeDtypeStruct(query_here.shape, query_here.dtype),
        scratch_shapes=[
            pltpu.VMEM(query_here.shape, query_here.dtype),
            near,
            near,
            far,
            far,
            part,
            part,
            pltpu.VMEM((2, share, nv * BS, head_dim), kind),
            operand,
            operand,
            state,
            state,
            state,
            pltpu.SemaphoreType.DMA((copies,)),
            pltpu.SemaphoreType.DMA((copies,)),
            pltpu.SemaphoreType.DMA((5,)),
        ],
        compiler_params=pltpu.CompilerParams(
            collective_id=0, has_side_effects=True, vmem_limit_bytes=56 * 1024 * 1024
        ),
    )(
        query_here,
        key_here.reshape(blocks, BS, width),
        value_here.reshape(blocks, BS, width),
        vertical_here,
        slash_here,
    )


def solution(mesh):
    in_specs = (
        P(("parts", "seq", "head"), None),
        P(("parts", "seq", "head"), None),
        P(("parts", "seq", "head"), None),
        P("parts", None),
        P("parts", None),
    )
    out_specs = P(("parts", "seq", "head"), None)
    return jax.shard_map(
        on_device, mesh=mesh, in_specs=in_specs, out_specs=out_specs, check_vma=False
    )
```

```python
import functools
import math

import jax
import jax.numpy as jnp
from jax import lax
from jax.experimental import pallas as pl
from jax.experimental.pallas import tpu as pltpu
from jax.sharding import PartitionSpec as P

BS = 64
SPAN = 8
MASKED = -1e30


MESH = pl.DeviceIdType.MESH


def gather_kernel(
    lanes,
    k_ref,
    v_ref,
    vertical,
    nk_ref,
    nv_ref,
    wk_ref,
    wv_ref,
    parts_k,
    parts_v,
    merged,
    send,
    recv,
    local,
):
    cores = lax.axis_size("head")
    levels = lax.axis_size("seq") * cores // lanes
    me = lax.axis_index(("seq", "head"))
    level, lane = me // lanes, me % lanes
    side, core = lane // cores, lane % cores
    blocks = k_ref.shape[0]
    share = wk_ref.shape[0] // lanes
    head_dim = wk_ref.shape[2]
    nv = vertical.shape[1]
    across, beside = me + cores * (1 - 2 * side), me + 1 - 2 * core
    above, below = me + lanes, me - lanes
    has_above, has_below = level < levels - 1, level > 0
    always = level >= 0

    def name(device):
        return {"seq": device // cores, "head": device % cores}

    peers = []
    for hop in range(1, lanes):
        peers.append((always, level * lanes + (lane + hop) % lanes))
    peers += [(has_above, above), (has_below, below)]
    barrier = pltpu.get_barrier_semaphore()
    for there, peer in peers:

        @pl.when(there)
        def _():
            pl.semaphore_signal(barrier, inc=1, device_id=name(peer), device_id_type=MESH)

    ends = jnp.where(has_above, 1, 0) + jnp.where(has_below, 1, 0)
    pl.semaphore_wait(barrier, lanes - 1 + ends)

    near = (nk_ref, nv_ref)
    own = (k_ref, v_ref)
    far = (wk_ref, wv_ref)
    parts = (parts_k, parts_v)
    count = [0]

    class Link:
        def __init__(self, sends, gets, source, target, device):
            at = count[0]
            count[0] += 1
            self.sends, self.gets = sends, gets
            self.copy = pltpu.make_async_remote_copy(
                src_ref=source,
                dst_ref=target,
                send_sem=send.at[at],
                recv_sem=recv.at[at],
                device_id=name(device),
                device_id_type=MESH,
            )

        def start(self, when=True):
            pl.when(self.sends & when)(lambda: self.copy.start())

        def arrived(self, when=True):
            pl.when(self.gets & when)(lambda: self.copy.wait_recv())

        def sent(self):
            pl.when(self.sends)(lambda: self.copy.wait_send())

    def slot(ref, distance):
        first = (lanes - distance) * blocks
        return ref.at[first : first + blocks]

    width = share * head_dim
    links = []

    def link(*args):
        links.append(Link(*args))
        return links[-1]

    split, up, out_own, out_far, pair_own, pair_far, pass_low, pass_high = ([] for _ in range(8))
    mine = pl.ds(lane * blocks, blocks)
    crossed = (side == 1) | has_below
    for kv in range(2):
        for hop in range(1, lanes):
            to = (lane + hop) % lanes
            columns = pl.ds(pl.multiple_of(to * width, width), width)
            split.append(
                link(
                    always,
                    always,
                    own[kv].at[:, :, columns],
                    parts[kv].at[mine],
                    level * lanes + to,
                )
            )
        old = slot(near[kv], lanes)
        middle = slot(near[kv], cores)
        first, third = slot(near[kv], 1), slot(near[kv], lanes - 1)
        up.append(link(has_above, has_below, own[kv], old, above))
        out_own.append(link(side == 0, side == 1, own[kv], middle, across))
        out_far.append(
            link((side == 1) & has_below, (side == 0) & has_below, old, middle, across)
        )
        pair_own.append(link(core == 0, core == 1, own[kv], first, beside))
        pair_far.append(link((core == 1) & has_below, (core == 0) & has_below, old, third, beside))
        pass_low.append(link((core == 0) & crossed, (core == 1) & crossed, middle, third, beside))
        pass_high.append(link((core == 1) & crossed, (core == 0) & crossed, middle, first, beside))

    rise, spread_pair, spread_across, spread_last = ([[], []] for _ in range(4))
    opposite = lane + cores * (1 - 2 * side)
    for kv in range(2):
        for h in range(share):
            here = far[kv].at[lane * share + h]
            there = far[kv].at[opposite * share + h]
            rise[kv].append(link(has_above, has_below, merged.at[kv, h], here, above))
            spread_pair[kv].append(link(has_below, has_below, here, here, beside))
            spread_across[kv].append(link(has_below, has_below, here, here, across))
            spread_last[kv].append(link(has_below, has_below, there, there, beside))

    for part in split[: lanes - 1]:
        part.start()
    up[0].start()
    for part in split[lanes - 1 :]:
        part.start()
    up[1].start(has_below)
    for kv in range(2):
        out_own[kv].start()
        pair_own[kv].start()
    my_columns = pl.ds(pl.multiple_of(lane * width, width), width)
    kept = []
    for kv in range(2):
        kept.append((own[kv].at[:, :, my_columns], parts[kv].at[mine]))
        kept.append((own[kv], slot(near[kv], 0)))
    kept = [
        pltpu.make_async_copy(source, target, local.at[i])
        for i, (source, target) in enumerate(kept)
    ]
    for copy in kept:
        copy.start()

    @pl.when(level == 0)
    def _():
        for kv in range(2):
            for h in range(share):
                far[kv][lane * share + h] = jnp.zeros(wk_ref.shape[1:], wk_ref.dtype)

    level_blocks = lanes * blocks
    def pass_on(kv, when=True):
        up[kv].arrived(when)
        out_far[kv].start(when)
        pair_far[kv].start(when)

    for part in split[: lanes - 1]:
        part.arrived()
    for copy in kept:
        copy.wait()
    pass_on(0)
    pass_on(1, level > 1)
    for kv in range(2):
        if kv == 1:
            for part in split[lanes - 1 :]:
                part.arrived()
        for h in range(share):
            rise[kv][h].arrived()
            for m in range(nv):
                at = vertical[lane * share + h, m] - level * level_blocks
                at_all = jnp.full((BS, head_dim), at, jnp.int32)
                inside = (at_all >= 0) & (at_all < level_blocks)
                at = jnp.minimum(jnp.maximum(at, 0), level_blocks - 1)
                rows = slice(m * BS, (m + 1) * BS)
                block = parts[kv][at][:, h * head_dim : (h + 1) * head_dim]
                before = far[kv][lane * share + h, rows, :]
                merged[kv, h, rows, :] = jnp.where(inside, block, before)
            rise[kv][h].start()
            spread_across[kv][h].start()
            spread_pair[kv][h].start()
    up[1].start(level == 0)
    pass_on(1, level == 1)
    for kv in range(2):
        out_own[kv].arrived()
        out_far[kv].arrived()
        pass_low[kv].start()
        pass_high[kv].start()
    for kv in range(2):
        for h in range(share):
            spread_across[kv][h].arrived()
            spread_last[kv][h].start()
    for kv in range(2):
        pair_own[kv].arrived()
        pair_far[kv].arrived()
        pass_low[kv].arrived()
        pass_high[kv].arrived()
        for h in range(share):
            spread_pair[kv][h].arrived()
    for kv in range(2):
        for h in range(share):
            spread_last[kv][h].arrived()
    for each in links:
        each.sent()


def gather(key_here, value_here, vertical_here):
    tokens, width = key_here.shape
    kv_heads, nv = vertical_here.shape
    head_dim = width // kv_heads
    lanes = -(-((SPAN - 1) * BS) // tokens)
    share = kv_heads // lanes
    vmem = pl.BlockSpec(memory_space=pltpu.VMEM)
    anywhere = pl.BlockSpec(memory_space=pl.ANY)
    blocks = tokens // BS
    near = jax.ShapeDtypeStruct(((lanes + 1) * blocks, BS, width), key_here.dtype)
    far = jax.ShapeDtypeStruct((kv_heads, nv * BS, head_dim), key_here.dtype)
    copies = 2 * (lanes - 1 + 7 + 4 * share)
    near_keys, near_values, far_keys, far_values = pl.pallas_call(
        functools.partial(gather_kernel, lanes),
        in_specs=[anywhere] * 2 + [pl.BlockSpec(memory_space=pltpu.SMEM)],
        out_specs=[vmem] * 4,
        out_shape=[near, near, far, far],
        scratch_shapes=[
            pltpu.VMEM((lanes * blocks, BS, share * head_dim), key_here.dtype),
            pltpu.VMEM((lanes * blocks, BS, share * head_dim), key_here.dtype),
            pltpu.VMEM((2, share, nv * BS, head_dim), key_here.dtype),
            pltpu.SemaphoreType.DMA((copies,)),
            pltpu.SemaphoreType.DMA((copies,)),
            pltpu.SemaphoreType.DMA((4,)),
        ],
        compiler_params=pltpu.CompilerParams(
            collective_id=0, has_side_effects=True, vmem_limit_bytes=56 * 1024 * 1024
        ),
    )(
        key_here.reshape(blocks, BS, width),
        value_here.reshape(blocks, BS, width),
        vertical_here,
    )
    return near_keys.reshape(-1, width), near_values.reshape(-1, width), far_keys, far_values


def attention_kernel(
    vertical, slash, q_ref, nk_ref, nv_ref, wk_ref, wv_ref, o_ref, kbuf, vbuf
):
    g = pl.program_id(0)
    position = lax.axis_index(("seq", "head"))
    tokens = q_ref.shape[0]
    head_dim = nk_ref.shape[1]
    groups = q_ref.shape[1] // head_dim
    block_count = tokens // BS
    window_blocks = nk_ref.shape[0] // BS
    back_blocks = window_blocks - block_count
    ns, nv = slash.shape[1], vertical.shape[1]
    window_first = position * block_count - back_blocks
    scale = math.log2(math.e) / math.sqrt(head_dim)

    row = lax.broadcasted_iota(jnp.int32, (BS, head_dim), 0)
    col = lax.broadcasted_iota(jnp.int32, (BS, head_dim), 1)
    token = jnp.where(row == col, 1.0, 0.0).astype(kbuf.dtype)

    @pl.when(g == 0)
    def _():
        vbuf[...] = jnp.ones_like(vbuf)
        later = jnp.where((col < BS) & (row > col), MASKED, 0.0).astype(kbuf.dtype)
        for b in range(block_count):
            kbuf[b, :BS, head_dim:] = later

    offsets = [slash[g, m] for m in range(ns)]
    columns = [vertical[g, m] for m in range(nv)]
    ordered = [jnp.int32(0)] + [
        jnp.where(offsets[m] == 0, offsets[0], offsets[m]) for m in range(1, ns)
    ]
    for b in range(block_count):
        query_block = position * block_count + b
        own = back_blocks + b
        for m in range(ns + nv):
            rows = pl.ds(m * BS, BS)
            if m < ns:
                active = ordered[m] <= query_block
                at = jnp.where(active, own - ordered[m], own)
                at = pl.multiple_of(at * BS, BS)
                key_block = nk_ref[pl.ds(at, BS), :]
                value_block = nv_ref[pl.ds(at, BS), :]
            else:
                j = columns[m - ns]
                active = j <= query_block
                for off in offsets:
                    active = active & (query_block - j != off)
                near = jnp.logical_not(active) | (j >= window_first)
                at = jnp.where(active & near, j - window_first, own)
                at = pl.multiple_of(at * BS, BS)
                far_rows = pl.ds((m - ns) * BS, BS)
                key_block = jnp.where(near, nk_ref[pl.ds(at, BS), :], wk_ref[0, far_rows, :])
                value_block = jnp.where(near, nv_ref[pl.ds(at, BS), :], wv_ref[0, far_rows, :])
            kbuf[b, rows, :head_dim] = key_block
            vbuf[b, rows, :head_dim] = value_block
            if m > 0:
                hidden = jnp.full((BS, head_dim), jnp.where(active, 0.0, MASKED), jnp.float32)
                kbuf[b, rows, head_dim:] = hidden.astype(kbuf.dtype)

    chunk = max(groups // 2, 1)

    def score(b, first):
        q_rows = slice(b * BS, (b + 1) * BS)
        query = jnp.concatenate(
            [
                jnp.concatenate([q_ref[q_rows, c * head_dim : (c + 1) * head_dim], token], axis=1)
                for c in range(first, first + chunk)
            ],
            axis=0,
        )
        return lax.dot_general(
            query, kbuf[b], (((1,), (1,)), ((), ())), preferred_element_type=jnp.float32
        )

    steps = [(b, first) for b in range(block_count) for first in range(0, groups, chunk)]
    ahead = score(*steps[0])
    for i, (b, first) in enumerate(steps):
        scores = ahead
        if i + 1 < len(steps):
            ahead = score(*steps[i + 1])
        row_max = jnp.max(scores, axis=-1, keepdims=True)
        weights = jnp.exp2((scores - row_max) * scale).astype(jnp.bfloat16)
        mixed = jnp.dot(weights, vbuf[b], preferred_element_type=jnp.float32)
        mixed = (mixed[:, :head_dim] / mixed[:, head_dim:]).astype(o_ref.dtype)
        for c in range(chunk):
            columns = slice((first + c) * head_dim, (first + c + 1) * head_dim)
            o_ref[b * BS : (b + 1) * BS, columns] = mixed[c * BS : (c + 1) * BS]


def attend(query_here, near_keys, near_values, far_keys, far_values, vertical_here, slash_here):
    length, width = query_here.shape
    kv_heads, nv = vertical_here.shape
    ns = slash_here.shape[1]
    head_dim = near_keys.shape[1] // kv_heads
    group_width = width // kv_heads
    block_count = length // BS
    near_spec = pl.BlockSpec((near_keys.shape[0], head_dim), lambda g, *_: (0, g))
    far_spec = pl.BlockSpec((1, nv * BS, head_dim), lambda g, *_: (g, 0, 0))
    row_spec = pl.BlockSpec((length, group_width), lambda g, *_: (0, g))
    slots = (ns + nv) * BS
    return pl.pallas_call(
        attention_kernel,
        grid_spec=pltpu.PrefetchScalarGridSpec(
            num_scalar_prefetch=2,
            grid=(kv_heads,),
            in_specs=[row_spec, near_spec, near_spec, far_spec, far_spec],
            out_specs=row_spec,
            scratch_shapes=[
                pltpu.VMEM((block_count, slots, 2 * head_dim), jnp.bfloat16),
                pltpu.VMEM((block_count, slots, 2 * head_dim), jnp.bfloat16),
            ],
        ),
        out_shape=jax.ShapeDtypeStruct((length, width), query_here.dtype),
        compiler_params=pltpu.CompilerParams(
            dimension_semantics=("arbitrary",), vmem_limit_bytes=58 * 1024 * 1024
        ),
        cost_estimate=pl.CostEstimate(
            flops=4 * length * width * slots,
            bytes_accessed=4 * length * width,
            transcendentals=length * width // head_dim * slots,
        ),
    )(vertical_here, slash_here, query_here, near_keys, near_values, far_keys, far_values)


def on_device(query_states, key_states, value_states, vertical_blocks, slash_offsets):
    gathered = gather(key_states, value_states, vertical_blocks)
    return attend(query_states, *gathered, vertical_blocks, slash_offsets)


def solution(mesh):
    in_specs = (
        P(("parts", "seq", "head"), None),
        P(("parts", "seq", "head"), None),
        P(("parts", "seq", "head"), None),
        P("parts", None),
        P("parts", None),
    )
    out_specs = P(("parts", "seq", "head"), None)
    return jax.shard_map(
        on_device, mesh=mesh, in_specs=in_specs, out_specs=out_specs, check_vma=False
    )
```

```python
import functools
import math

import jax
import jax.numpy as jnp
from jax import lax
from jax.experimental import pallas as pl
from jax.experimental.pallas import tpu as pltpu
from jax.sharding import PartitionSpec as P

BS = 64
SPAN = 8
MASKED = -1e30


MESH = pl.DeviceIdType.MESH


def gather_kernel(
    lanes,
    k_ref,
    v_ref,
    vertical,
    nk_ref,
    nv_ref,
    wk_ref,
    wv_ref,
    parts_k,
    parts_v,
    merged,
    send,
    recv,
    local,
):
    cores = lax.axis_size("head")
    levels = lax.axis_size("seq") * cores // lanes
    me = lax.axis_index(("seq", "head"))
    level, lane = me // lanes, me % lanes
    side, core = lane // cores, lane % cores
    blocks = k_ref.shape[0]
    share = wk_ref.shape[0] // lanes
    head_dim = wk_ref.shape[2]
    nv = vertical.shape[1]
    across, beside = me + cores * (1 - 2 * side), me + 1 - 2 * core
    above, below = me + lanes, me - lanes
    has_above, has_below = level < levels - 1, level > 0
    always = level >= 0

    def name(device):
        return {"seq": device // cores, "head": device % cores}

    peers = []
    for hop in range(1, lanes):
        peers.append((always, level * lanes + (lane + hop) % lanes))
    peers += [(has_above, above), (has_below, below)]
    barrier = pltpu.get_barrier_semaphore()
    for there, peer in peers:

        @pl.when(there)
        def _():
            pl.semaphore_signal(barrier, inc=1, device_id=name(peer), device_id_type=MESH)

    ends = jnp.where(has_above, 1, 0) + jnp.where(has_below, 1, 0)
    pl.semaphore_wait(barrier, lanes - 1 + ends)

    near = (nk_ref, nv_ref)
    own = (k_ref, v_ref)
    far = (wk_ref, wv_ref)
    parts = (parts_k, parts_v)
    count = [0]

    class Link:
        def __init__(self, sends, gets, source, target, device):
            at = count[0]
            count[0] += 1
            self.sends, self.gets = sends, gets
            self.copy = pltpu.make_async_remote_copy(
                src_ref=source,
                dst_ref=target,
                send_sem=send.at[at],
                recv_sem=recv.at[at],
                device_id=name(device),
                device_id_type=MESH,
            )

        def start(self, when=True):
            pl.when(self.sends & when)(lambda: self.copy.start())

        def arrived(self, when=True):
            pl.when(self.gets & when)(lambda: self.copy.wait_recv())

        def sent(self):
            pl.when(self.sends)(lambda: self.copy.wait_send())

    def slot(ref, distance):
        first = (lanes - distance) * blocks
        return ref.at[first : first + blocks]

    width = share * head_dim
    links = []

    def link(*args):
        links.append(Link(*args))
        return links[-1]

    split, up, out_own, out_far, pair_own, pair_far, pass_low, pass_high = ([] for _ in range(8))
    mine = pl.ds(lane * blocks, blocks)
    crossed = (side == 1) | has_below
    for kv in range(2):
        for hop in range(1, lanes):
            to = (lane + hop) % lanes
            columns = pl.ds(pl.multiple_of(to * width, width), width)
            split.append(
                link(
                    always,
                    always,
                    own[kv].at[:, :, columns],
                    parts[kv].at[mine],
                    level * lanes + to,
                )
            )
        old = slot(near[kv], lanes)
        middle = slot(near[kv], cores)
        first, third = slot(near[kv], 1), slot(near[kv], lanes - 1)
        up.append(link(has_above, has_below, own[kv], old, above))
        out_own.append(link(side == 0, side == 1, own[kv], middle, across))
        out_far.append(
            link((side == 1) & has_below, (side == 0) & has_below, old, middle, across)
        )
        pair_own.append(link(core == 0, core == 1, own[kv], first, beside))
        pair_far.append(link((core == 1) & has_below, (core == 0) & has_below, old, third, beside))
        pass_low.append(link((core == 0) & crossed, (core == 1) & crossed, middle, third, beside))
        pass_high.append(link((core == 1) & crossed, (core == 0) & crossed, middle, first, beside))

    rise, spread_pair, spread_across, spread_last = ([[], []] for _ in range(4))
    opposite = lane + cores * (1 - 2 * side)
    for kv in range(2):
        for h in range(share):
            here = far[kv].at[lane * share + h]
            there = far[kv].at[opposite * share + h]
            rise[kv].append(link(has_above, has_below, merged.at[kv, h], here, above))
            spread_pair[kv].append(link(has_below, has_below, here, here, beside))
            spread_across[kv].append(link(has_below, has_below, here, here, across))
            spread_last[kv].append(link(has_below, has_below, there, there, beside))

    for part in split[: lanes - 1]:
        part.start()
    up[0].start()
    for part in split[lanes - 1 :]:
        part.start()
    up[1].start(has_below)
    for kv in range(2):
        out_own[kv].start()
        pair_own[kv].start()
    my_columns = pl.ds(pl.multiple_of(lane * width, width), width)
    kept = []
    for kv in range(2):
        kept.append((own[kv].at[:, :, my_columns], parts[kv].at[mine]))
        kept.append((own[kv], slot(near[kv], 0)))
    kept = [
        pltpu.make_async_copy(source, target, local.at[i])
        for i, (source, target) in enumerate(kept)
    ]
    for copy in kept:
        copy.start()

    @pl.when(level == 0)
    def _():
        for kv in range(2):
            for h in range(share):
                far[kv][lane * share + h] = jnp.zeros(wk_ref.shape[1:], wk_ref.dtype)

    level_blocks = lanes * blocks
    def pass_on(kv, when=True):
        up[kv].arrived(when)
        out_far[kv].start(when)
        pair_far[kv].start(when)

    for part in split[: lanes - 1]:
        part.arrived()
    for copy in kept:
        copy.wait()
    pass_on(0)
    pass_on(1, level > 1)
    for kv in range(2):
        if kv == 1:
            for part in split[lanes - 1 :]:
                part.arrived()
        for h in range(share):
            rise[kv][h].arrived()
            for m in range(nv):
                at = vertical[lane * share + h, m] - level * level_blocks
                at_all = jnp.full((BS, head_dim), at, jnp.int32)
                inside = (at_all >= 0) & (at_all < level_blocks)
                at = jnp.minimum(jnp.maximum(at, 0), level_blocks - 1)
                rows = slice(m * BS, (m + 1) * BS)
                block = parts[kv][at][:, h * head_dim : (h + 1) * head_dim]
                before = far[kv][lane * share + h, rows, :]
                merged[kv, h, rows, :] = jnp.where(inside, block, before)
            rise[kv][h].start()
            spread_across[kv][h].start()
            spread_pair[kv][h].start()
    up[1].start(level == 0)
    pass_on(1, level == 1)
    for kv in range(2):
        out_own[kv].arrived()
        out_far[kv].arrived()
        pass_low[kv].start()
        pass_high[kv].start()
    for kv in range(2):
        for h in range(share):
            spread_across[kv][h].arrived()
            spread_last[kv][h].start()
    for kv in range(2):
        pair_own[kv].arrived()
        pair_far[kv].arrived()
        pass_low[kv].arrived()
        pass_high[kv].arrived()
        for h in range(share):
            spread_pair[kv][h].arrived()
    for kv in range(2):
        for h in range(share):
            spread_last[kv][h].arrived()
    for each in links:
        each.sent()


def gather(key_here, value_here, vertical_here):
    tokens, width = key_here.shape
    kv_heads, nv = vertical_here.shape
    head_dim = width // kv_heads
    lanes = -(-((SPAN - 1) * BS) // tokens)
    share = kv_heads // lanes
    vmem = pl.BlockSpec(memory_space=pltpu.VMEM)
    anywhere = pl.BlockSpec(memory_space=pl.ANY)
    blocks = tokens // BS
    near = jax.ShapeDtypeStruct(((lanes + 1) * blocks, BS, width), key_here.dtype)
    far = jax.ShapeDtypeStruct((kv_heads, nv * BS, head_dim), key_here.dtype)
    copies = 2 * (lanes - 1 + 7 + 4 * share)
    near_keys, near_values, far_keys, far_values = pl.pallas_call(
        functools.partial(gather_kernel, lanes),
        in_specs=[anywhere] * 2 + [pl.BlockSpec(memory_space=pltpu.SMEM)],
        out_specs=[vmem] * 4,
        out_shape=[near, near, far, far],
        scratch_shapes=[
            pltpu.VMEM((lanes * blocks, BS, share * head_dim), key_here.dtype),
            pltpu.VMEM((lanes * blocks, BS, share * head_dim), key_here.dtype),
            pltpu.VMEM((2, share, nv * BS, head_dim), key_here.dtype),
            pltpu.SemaphoreType.DMA((copies,)),
            pltpu.SemaphoreType.DMA((copies,)),
            pltpu.SemaphoreType.DMA((4,)),
        ],
        compiler_params=pltpu.CompilerParams(
            collective_id=0, has_side_effects=True, vmem_limit_bytes=56 * 1024 * 1024
        ),
    )(
        key_here.reshape(blocks, BS, width),
        value_here.reshape(blocks, BS, width),
        vertical_here,
    )
    return near_keys.reshape(-1, width), near_values.reshape(-1, width), far_keys, far_values


def attention_kernel(
    vertical, slash, q_ref, nk_ref, nv_ref, wk_ref, wv_ref, o_ref, kbuf, vbuf
):
    step = pl.program_id(0)
    position = lax.axis_index(("seq", "head"))
    tokens = q_ref.shape[0]
    heads, head_dim = wk_ref.shape[0], wk_ref.shape[2]
    groups = q_ref.shape[1] // (heads * head_dim)
    block_count = tokens // BS
    window_blocks = nk_ref.shape[0] // BS
    back_blocks = window_blocks - block_count
    ns, nv = slash.shape[1], vertical.shape[1]
    window_first = position * block_count - back_blocks
    scale = math.log2(math.e) / math.sqrt(head_dim)

    row = lax.broadcasted_iota(jnp.int32, (BS, head_dim), 0)
    col = lax.broadcasted_iota(jnp.int32, (BS, head_dim), 1)
    token = jnp.where(row == col, 1.0, 0.0).astype(kbuf.dtype)

    @pl.when(step == 0)
    def _():
        vbuf[...] = jnp.ones_like(vbuf)
        later = jnp.where((col < BS) & (row > col), MASKED, 0.0).astype(kbuf.dtype)
        for n in range(heads * block_count):
            kbuf[n, :BS, head_dim:] = later

    def fill(head, b):
        g = step * heads + head
        n = head * block_count + b
        offsets = [slash[g, m] for m in range(ns)]
        ordered = [jnp.int32(0)] + [
            jnp.where(offsets[m] == 0, offsets[0], offsets[m]) for m in range(1, ns)
        ]
        lanes = slice(head * head_dim, (head + 1) * head_dim)
        query_block = position * block_count + b
        own = back_blocks + b
        for m in range(ns + nv):
            rows = pl.ds(m * BS, BS)
            if m < ns:
                active = ordered[m] <= query_block
                at = jnp.where(active, own - ordered[m], own)
                at = pl.multiple_of(at * BS, BS)
                key_block = nk_ref[pl.ds(at, BS), lanes]
                value_block = nv_ref[pl.ds(at, BS), lanes]
            else:
                j = vertical[g, m - ns]
                active = j <= query_block
                for off in offsets:
                    active = active & (query_block - j != off)
                near = jnp.logical_not(active) | (j >= window_first)
                at = jnp.where(active & near, j - window_first, own)
                at = pl.multiple_of(at * BS, BS)
                far_rows = pl.ds((m - ns) * BS, BS)
                key_block = jnp.where(near, nk_ref[pl.ds(at, BS), lanes], wk_ref[head, far_rows, :])
                value_block = jnp.where(
                    near, nv_ref[pl.ds(at, BS), lanes], wv_ref[head, far_rows, :]
                )
            kbuf[n, rows, :head_dim] = key_block
            vbuf[n, rows, :head_dim] = value_block
            if m > 0:
                hidden = jnp.full((BS, head_dim), jnp.where(active, 0.0, MASKED), jnp.float32)
                kbuf[n, rows, head_dim:] = hidden.astype(kbuf.dtype)

    chunk = max(groups // 2, 1)

    def columns_of(head, c):
        first = (head * groups + c) * head_dim
        return slice(first, first + head_dim)

    def score(head, b, first):
        if first == 0:
            fill(head, b)
        q_rows = slice(b * BS, (b + 1) * BS)
        query = jnp.concatenate(
            [
                jnp.concatenate([q_ref[q_rows, columns_of(head, c)], token], axis=1)
                for c in range(first, first + chunk)
            ],
            axis=0,
        )
        return lax.dot_general(
            query,
            kbuf[head * block_count + b],
            (((1,), (1,)), ((), ())),
            preferred_element_type=jnp.float32,
        )

    steps = [
        (head, b, first)
        for head in range(heads)
        for b in range(block_count)
        for first in range(0, groups, chunk)
    ]
    ahead = score(*steps[0])
    for i, (head, b, first) in enumerate(steps):
        scores = ahead
        if i + 1 < len(steps):
            ahead = score(*steps[i + 1])
        row_max = jnp.max(scores, axis=-1, keepdims=True)
        weights = jnp.exp2((scores - row_max) * scale).astype(jnp.bfloat16)
        mixed = jnp.dot(
            weights, vbuf[head * block_count + b], preferred_element_type=jnp.float32
        )
        mixed = (mixed[:, :head_dim] / mixed[:, head_dim:]).astype(o_ref.dtype)
        for c in range(chunk):
            o_ref[b * BS : (b + 1) * BS, columns_of(head, first + c)] = mixed[
                c * BS : (c + 1) * BS
            ]


def attend(query_here, near_keys, near_values, far_keys, far_values, vertical_here, slash_here):
    length, width = query_here.shape
    kv_heads, nv = vertical_here.shape
    ns = slash_here.shape[1]
    head_dim = near_keys.shape[1] // kv_heads
    group_width = width // kv_heads
    block_count = length // BS
    heads = 2 if kv_heads % 2 == 0 else 1
    near_spec = pl.BlockSpec((near_keys.shape[0], heads * head_dim), lambda g, *_: (0, g))
    far_spec = pl.BlockSpec((heads, nv * BS, head_dim), lambda g, *_: (g, 0, 0))
    row_spec = pl.BlockSpec((length, heads * group_width), lambda g, *_: (0, g))
    slots = (ns + nv) * BS
    return pl.pallas_call(
        attention_kernel,
        grid_spec=pltpu.PrefetchScalarGridSpec(
            num_scalar_prefetch=2,
            grid=(kv_heads // heads,),
            in_specs=[row_spec, near_spec, near_spec, far_spec, far_spec],
            out_specs=row_spec,
            scratch_shapes=[
                pltpu.VMEM((heads * block_count, slots, 2 * head_dim), jnp.bfloat16),
                pltpu.VMEM((heads * block_count, slots, 2 * head_dim), jnp.bfloat16),
            ],
        ),
        out_shape=jax.ShapeDtypeStruct((length, width), query_here.dtype),
        compiler_params=pltpu.CompilerParams(
            dimension_semantics=("arbitrary",), vmem_limit_bytes=58 * 1024 * 1024
        ),
        cost_estimate=pl.CostEstimate(
            flops=4 * length * width * slots,
            bytes_accessed=4 * length * width,
            transcendentals=length * width // head_dim * slots,
        ),
    )(vertical_here, slash_here, query_here, near_keys, near_values, far_keys, far_values)


def on_device(query_states, key_states, value_states, vertical_blocks, slash_offsets):
    gathered = gather(key_states, value_states, vertical_blocks)
    return attend(query_states, *gathered, vertical_blocks, slash_offsets)


def solution(mesh):
    in_specs = (
        P(("parts", "seq", "head"), None),
        P(("parts", "seq", "head"), None),
        P(("parts", "seq", "head"), None),
        P("parts", None),
        P("parts", None),
    )
    out_specs = P(("parts", "seq", "head"), None)
    return jax.shard_map(
        on_device, mesh=mesh, in_specs=in_specs, out_specs=out_specs, check_vma=False
    )
```

```python
import functools
import math

import jax
import jax.numpy as jnp
from jax import lax
from jax.experimental import pallas as pl
from jax.experimental.pallas import tpu as pltpu
from jax.sharding import PartitionSpec as P

BS = 64
SPAN = 8
MASKED = -1e30


MESH = pl.DeviceIdType.MESH


def gather_kernel(
    lanes,
    k_ref,
    v_ref,
    vertical,
    nk_ref,
    nv_ref,
    wk_ref,
    wv_ref,
    parts_k,
    parts_v,
    merged,
    send,
    recv,
    local,
):
    cores = lax.axis_size("head")
    levels = lax.axis_size("seq") * cores // lanes
    me = lax.axis_index(("seq", "head"))
    level, lane = me // lanes, me % lanes
    side, core = lane // cores, lane % cores
    blocks = k_ref.shape[0]
    share = wk_ref.shape[0] // lanes
    head_dim = wk_ref.shape[2]
    nv = vertical.shape[1]
    across, beside = me + cores * (1 - 2 * side), me + 1 - 2 * core
    above, below = me + lanes, me - lanes
    has_above, has_below = level < levels - 1, level > 0
    always = level >= 0

    def name(device):
        return {"seq": device // cores, "head": device % cores}

    peers = []
    for hop in range(1, lanes):
        peers.append((always, level * lanes + (lane + hop) % lanes))
    peers += [(has_above, above), (has_below, below)]
    barrier = pltpu.get_barrier_semaphore()
    for there, peer in peers:

        @pl.when(there)
        def _():
            pl.semaphore_signal(barrier, inc=1, device_id=name(peer), device_id_type=MESH)

    ends = jnp.where(has_above, 1, 0) + jnp.where(has_below, 1, 0)
    pl.semaphore_wait(barrier, lanes - 1 + ends)

    near = (nk_ref, nv_ref)
    own = (k_ref, v_ref)
    far = (wk_ref, wv_ref)
    parts = (parts_k, parts_v)
    count = [0]

    class Link:
        def __init__(self, sends, gets, source, target, device):
            at = count[0]
            count[0] += 1
            self.sends, self.gets = sends, gets
            self.copy = pltpu.make_async_remote_copy(
                src_ref=source,
                dst_ref=target,
                send_sem=send.at[at],
                recv_sem=recv.at[at],
                device_id=name(device),
                device_id_type=MESH,
            )

        def start(self, when=True):
            pl.when(self.sends & when)(lambda: self.copy.start())

        def arrived(self, when=True):
            pl.when(self.gets & when)(lambda: self.copy.wait_recv())

        def sent(self):
            pl.when(self.sends)(lambda: self.copy.wait_send())

    def slot(ref, distance):
        first = (lanes - distance) * blocks
        return ref.at[first : first + blocks]

    width = share * head_dim
    links = []

    def link(*args):
        links.append(Link(*args))
        return links[-1]

    split, up, out_own, out_far, pair_own, pair_far, pass_low, pass_high = ([] for _ in range(8))
    mine = pl.ds(lane * blocks, blocks)
    crossed = (side == 1) | has_below
    for kv in range(2):
        for hop in range(1, lanes):
            to = (lane + hop) % lanes
            columns = pl.ds(pl.multiple_of(to * width, width), width)
            split.append(
                link(
                    always,
                    always,
                    own[kv].at[:, :, columns],
                    parts[kv].at[mine],
                    level * lanes + to,
                )
            )
        old = slot(near[kv], lanes)
        middle = slot(near[kv], cores)
        first, third = slot(near[kv], 1), slot(near[kv], lanes - 1)
        up.append(link(has_above, has_below, own[kv], old, above))
        out_own.append(link(side == 0, side == 1, own[kv], middle, across))
        out_far.append(
            link((side == 1) & has_below, (side == 0) & has_below, old, middle, across)
        )
        pair_own.append(link(core == 0, core == 1, own[kv], first, beside))
        pair_far.append(link((core == 1) & has_below, (core == 0) & has_below, old, third, beside))
        pass_low.append(link((core == 0) & crossed, (core == 1) & crossed, middle, third, beside))
        pass_high.append(link((core == 1) & crossed, (core == 0) & crossed, middle, first, beside))

    rise, spread_pair, spread_across, spread_last = ([[], []] for _ in range(4))
    opposite = lane + cores * (1 - 2 * side)
    for kv in range(2):
        for h in range(share):
            here = far[kv].at[lane * share + h]
            there = far[kv].at[opposite * share + h]
            rise[kv].append(link(has_above, has_below, merged.at[kv, h], here, above))
            spread_pair[kv].append(link(has_below, has_below, here, here, beside))
            spread_across[kv].append(link(has_below, has_below, here, here, across))
            spread_last[kv].append(link(has_below, has_below, there, there, beside))

    for part in split[: lanes - 1]:
        part.start()
    up[0].start()
    for part in split[lanes - 1 :]:
        part.start()
    up[1].start(has_below)
    for kv in range(2):
        out_own[kv].start()
        pair_own[kv].start()
    my_columns = pl.ds(pl.multiple_of(lane * width, width), width)
    kept = []
    for kv in range(2):
        kept.append((own[kv].at[:, :, my_columns], parts[kv].at[mine]))
        kept.append((own[kv], slot(near[kv], 0)))
    kept = [
        pltpu.make_async_copy(source, target, local.at[i])
        for i, (source, target) in enumerate(kept)
    ]
    for copy in kept:
        copy.start()

    @pl.when(level == 0)
    def _():
        for kv in range(2):
            for h in range(share):
                far[kv][lane * share + h] = jnp.zeros(wk_ref.shape[1:], wk_ref.dtype)

    level_blocks = lanes * blocks
    def pass_on(kv, when=True):
        up[kv].arrived(when)
        out_far[kv].start(when)
        pair_far[kv].start(when)

    for part in split[: lanes - 1]:
        part.arrived()
    for copy in kept:
        copy.wait()
    pass_on(0)
    pass_on(1, level > 1)
    for kv in range(2):
        if kv == 1:
            for part in split[lanes - 1 :]:
                part.arrived()
        for h in range(share):
            rise[kv][h].arrived()
            for m in range(nv):
                at = vertical[lane * share + h, m] - level * level_blocks
                at_all = jnp.full((BS, head_dim), at, jnp.int32)
                inside = (at_all >= 0) & (at_all < level_blocks)
                at = jnp.minimum(jnp.maximum(at, 0), level_blocks - 1)
                rows = slice(m * BS, (m + 1) * BS)
                block = parts[kv][at][:, h * head_dim : (h + 1) * head_dim]
                before = far[kv][lane * share + h, rows, :]
                merged[kv, h, rows, :] = jnp.where(inside, block, before)
            rise[kv][h].start()
            spread_across[kv][h].start()
            spread_pair[kv][h].start()
    up[1].start(level == 0)
    pass_on(1, level == 1)
    for kv in range(2):
        out_own[kv].arrived()
        out_far[kv].arrived()
        pass_low[kv].start()
        pass_high[kv].start()
    for kv in range(2):
        for h in range(share):
            spread_across[kv][h].arrived()
            spread_last[kv][h].start()
    for kv in range(2):
        pair_own[kv].arrived()
        pair_far[kv].arrived()
        pass_low[kv].arrived()
        pass_high[kv].arrived()
        for h in range(share):
            spread_pair[kv][h].arrived()
    for kv in range(2):
        for h in range(share):
            spread_last[kv][h].arrived()
    for each in links:
        each.sent()


def gather(key_here, value_here, vertical_here):
    tokens, width = key_here.shape
    kv_heads, nv = vertical_here.shape
    head_dim = width // kv_heads
    lanes = -(-((SPAN - 1) * BS) // tokens)
    share = kv_heads // lanes
    vmem = pl.BlockSpec(memory_space=pltpu.VMEM)
    anywhere = pl.BlockSpec(memory_space=pl.ANY)
    blocks = tokens // BS
    near = jax.ShapeDtypeStruct(((lanes + 1) * blocks, BS, width), key_here.dtype)
    far = jax.ShapeDtypeStruct((kv_heads, nv * BS, head_dim), key_here.dtype)
    copies = 2 * (lanes - 1 + 7 + 4 * share)
    near_keys, near_values, far_keys, far_values = pl.pallas_call(
        functools.partial(gather_kernel, lanes),
        in_specs=[anywhere] * 2 + [pl.BlockSpec(memory_space=pltpu.SMEM)],
        out_specs=[vmem] * 4,
        out_shape=[near, near, far, far],
        scratch_shapes=[
            pltpu.VMEM((lanes * blocks, BS, share * head_dim), key_here.dtype),
            pltpu.VMEM((lanes * blocks, BS, share * head_dim), key_here.dtype),
            pltpu.VMEM((2, share, nv * BS, head_dim), key_here.dtype),
            pltpu.SemaphoreType.DMA((copies,)),
            pltpu.SemaphoreType.DMA((copies,)),
            pltpu.SemaphoreType.DMA((4,)),
        ],
        compiler_params=pltpu.CompilerParams(
            collective_id=0, has_side_effects=True, vmem_limit_bytes=56 * 1024 * 1024
        ),
    )(
        key_here.reshape(blocks, BS, width),
        value_here.reshape(blocks, BS, width),
        vertical_here,
    )
    return near_keys.reshape(-1, width), near_values.reshape(-1, width), far_keys, far_values


def attention_kernel(
    vertical, slash, q_ref, nk_ref, nv_ref, wk_ref, wv_ref, o_ref, kbuf, vbuf
):
    step = pl.program_id(0)
    position = lax.axis_index(("seq", "head"))
    tokens = q_ref.shape[0]
    heads, head_dim = wk_ref.shape[0], wk_ref.shape[2]
    groups = q_ref.shape[1] // (heads * head_dim)
    block_count = tokens // BS
    window_blocks = nk_ref.shape[0] // BS
    back_blocks = window_blocks - block_count
    ns, nv = slash.shape[1], vertical.shape[1]
    window_first = position * block_count - back_blocks
    scale = math.log2(math.e) / math.sqrt(head_dim)

    row = lax.broadcasted_iota(jnp.int32, (BS, head_dim), 0)
    col = lax.broadcasted_iota(jnp.int32, (BS, head_dim), 1)
    token = jnp.where(row == col, 1.0, 0.0).astype(kbuf.dtype)

    @pl.when(step == 0)
    def _():
        vbuf[...] = jnp.ones_like(vbuf)
        later = jnp.where((col < BS) & (row > col), MASKED, 0.0).astype(kbuf.dtype)
        for n in range(heads * block_count):
            kbuf[n, :BS, head_dim:] = later

    def fill(head, b):
        g = step * heads + head
        n = head * block_count + b
        offsets = [slash[g, m] for m in range(ns)]
        ordered = [jnp.int32(0)] + [
            jnp.where(offsets[m] == 0, offsets[0], offsets[m]) for m in range(1, ns)
        ]
        lanes = slice(head * head_dim, (head + 1) * head_dim)
        query_block = position * block_count + b
        own = back_blocks + b
        for m in range(ns + nv):
            rows = pl.ds(m * BS, BS)
            if m < ns:
                active = ordered[m] <= query_block
                at = jnp.where(active, own - ordered[m], own)
                at = pl.multiple_of(at * BS, BS)
                key_block = nk_ref[pl.ds(at, BS), lanes]
                value_block = nv_ref[pl.ds(at, BS), lanes]
            else:
                j = vertical[g, m - ns]
                active = j <= query_block
                for off in offsets:
                    active = active & (query_block - j != off)
                near = jnp.logical_not(active) | (j >= window_first)
                at = jnp.where(active & near, j - window_first, own)
                at = pl.multiple_of(at * BS, BS)
                far_rows = pl.ds((m - ns) * BS, BS)
                key_block = jnp.where(near, nk_ref[pl.ds(at, BS), lanes], wk_ref[head, far_rows, :])
                value_block = jnp.where(
                    near, nv_ref[pl.ds(at, BS), lanes], wv_ref[head, far_rows, :]
                )
            kbuf[n, rows, :head_dim] = key_block
            vbuf[n, rows, :head_dim] = value_block
            if m > 0:
                hidden = jnp.full((BS, head_dim), jnp.where(active, 0.0, MASKED), jnp.float32)
                kbuf[n, rows, head_dim:] = hidden.astype(kbuf.dtype)

    chunk = max(groups // 2, 1)

    def columns_of(head, c):
        first = (head * groups + c) * head_dim
        return slice(first, first + head_dim)

    def score(head, b, first):
        if first == 0:
            fill(head, b)
        q_rows = slice(b * BS, (b + 1) * BS)
        query = jnp.concatenate(
            [
                jnp.concatenate([q_ref[q_rows, columns_of(head, c)], token], axis=1)
                for c in range(first, first + chunk)
            ],
            axis=0,
        )
        return lax.dot_general(
            query,
            kbuf[head * block_count + b],
            (((1,), (1,)), ((), ())),
            preferred_element_type=jnp.float32,
        )

    steps = [
        (head, b, first)
        for head in range(heads)
        for b in range(block_count)
        for first in range(0, groups, chunk)
    ]
    ahead = score(*steps[0])
    for i, (head, b, first) in enumerate(steps):
        scores = ahead
        if i + 1 < len(steps):
            ahead = score(*steps[i + 1])
        row_max = jnp.max(scores, axis=-1, keepdims=True)
        weights = jnp.exp2((scores - row_max) * scale).astype(jnp.bfloat16)
        mixed = jnp.dot(
            weights, vbuf[head * block_count + b], preferred_element_type=jnp.float32
        )
        row_total = mixed[:, head_dim:]
        inverse = pl.reciprocal(row_total, approx=True)
        inverse = inverse * (2.0 - row_total * inverse)
        mixed = (mixed[:, :head_dim] * inverse).astype(o_ref.dtype)
        for c in range(chunk):
            o_ref[b * BS : (b + 1) * BS, columns_of(head, first + c)] = mixed[
                c * BS : (c + 1) * BS
            ]


def attend(query_here, near_keys, near_values, far_keys, far_values, vertical_here, slash_here):
    length, width = query_here.shape
    kv_heads, nv = vertical_here.shape
    ns = slash_here.shape[1]
    head_dim = near_keys.shape[1] // kv_heads
    group_width = width // kv_heads
    block_count = length // BS
    heads = 2 if kv_heads % 2 == 0 else 1
    near_spec = pl.BlockSpec((near_keys.shape[0], heads * head_dim), lambda g, *_: (0, g))
    far_spec = pl.BlockSpec((heads, nv * BS, head_dim), lambda g, *_: (g, 0, 0))
    row_spec = pl.BlockSpec((length, heads * group_width), lambda g, *_: (0, g))
    slots = (ns + nv) * BS
    return pl.pallas_call(
        attention_kernel,
        grid_spec=pltpu.PrefetchScalarGridSpec(
            num_scalar_prefetch=2,
            grid=(kv_heads // heads,),
            in_specs=[row_spec, near_spec, near_spec, far_spec, far_spec],
            out_specs=row_spec,
            scratch_shapes=[
                pltpu.VMEM((heads * block_count, slots, 2 * head_dim), jnp.bfloat16),
                pltpu.VMEM((heads * block_count, slots, 2 * head_dim), jnp.bfloat16),
            ],
        ),
        out_shape=jax.ShapeDtypeStruct((length, width), query_here.dtype),
        compiler_params=pltpu.CompilerParams(
            dimension_semantics=("arbitrary",), vmem_limit_bytes=58 * 1024 * 1024
        ),
        cost_estimate=pl.CostEstimate(
            flops=4 * length * width * slots,
            bytes_accessed=4 * length * width,
            transcendentals=length * width // head_dim * slots,
        ),
    )(vertical_here, slash_here, query_here, near_keys, near_values, far_keys, far_values)


def on_device(query_states, key_states, value_states, vertical_blocks, slash_offsets):
    gathered = gather(key_states, value_states, vertical_blocks)
    return attend(query_states, *gathered, vertical_blocks, slash_offsets)


def solution(mesh):
    in_specs = (
        P(("parts", "seq", "head"), None),
        P(("parts", "seq", "head"), None),
        P(("parts", "seq", "head"), None),
        P("parts", None),
        P("parts", None),
    )
    out_specs = P(("parts", "seq", "head"), None)
    return jax.shard_map(
        on_device, mesh=mesh, in_specs=in_specs, out_specs=out_specs, check_vma=False
    )
```
